128 devices in a mesh: gx: 4 (over y_lo, core), gy: 4 (over z), gz: 8 (over y_hi, x).
Axes of the slice: x: 4, y: 4 (y_hi: 2, y_lo: 2; y = y_hi * 2 + y_lo), z: 4, core: 2. Of those that a mesh axis runs over, the one named last changes fastest.
Arguments:
- right_sides: float32 [6, 128, 128, 1024], P(None, 'gx', 'gy', 'gz'), may hold values from -6 to 6
- permeability: float32 [128, 128, 1024], P('gx', 'gy', 'gz'), may hold values from 0.1 to 10
Outputs:
- basis_q: float32 [24, 128, 128, 1024], P(None, 'gx', 'gy', 'gz')
- factor_r: float32 [24, 24], replicated
The draws below stay inside these ranges and needn't reach their ends.
All inputs are finite; a program needn't handle non-finite values.
Results may differ from the reference program's by a relative error of at most 0.00012.
Values sent between devices are 32-bit elements; how exact they have to be, the bound alone decides.
A program may use at most 128 MiB of HBM per device.

```python
import math
import jax
import jax.numpy as jnp
from jax import lax

NRHS = 6
SSTEP = 3
NCOL = 24
NX = 128
NY = 128
NZ = 1024
CELLS = 16777216


def steps_of(stream_key, dims, pieces, smallest, high):
    factor_of = 1.0
    for axis_at, parts in pieces:
        draws = jax.random.uniform(jax.random.fold_in(jax.random.fold_in(stream_key, 6), axis_at), (parts,), jnp.float32, smallest / len(pieces), high / len(pieces))
        factor_of = factor_of * jnp.repeat(jnp.exp(draws), dims[axis_at] // parts).reshape((-1,) + (1,) * (len(dims) - 1 - axis_at))
    return factor_of


def centred(key, dims, deviation, bound, cuts=(), dtype=jnp.bfloat16):
    entries = deviation * jax.random.normal(key, dims, jnp.float32)
    if cuts:
        entries = entries * steps_of(key, dims, cuts, -0.22, 0.18)
    return jnp.clip(entries, -bound, bound).astype(dtype)


def setup_inputs(seed: int = 0) -> dict:
    streams_of = jax.random.split(jax.random.key(seed), 3)
    right_sides = centred(streams_of[0], (NRHS, NX, NY, NZ), 1.0, 6.0, ((1, 4), (2, 4), (3, 8)), jnp.float32)
    permeability = jnp.clip(jnp.exp(math.log(10.0) - 4.6051702 * jax.random.uniform(streams_of[1], (NX, NY, NZ), jnp.float32) ** steps_of(streams_of[1], (NX, NY, NZ), ((0, 4), (1, 4), (2, 8)), -0.2, 0.2)), 0.1, 10.0)
    return dict(right_sides=right_sides, permeability=permeability)


def face_weights(kappa_pad):
    center = kappa_pad[1:-1, 1:-1, 1:-1]
    others = [kappa_pad[2:, 1:-1, 1:-1], kappa_pad[:-2, 1:-1, 1:-1], kappa_pad[1:-1, 2:, 1:-1], kappa_pad[1:-1, :-2, 1:-1], kappa_pad[1:-1, 1:-1, 2:], kappa_pad[1:-1, 1:-1, :-2]]
    face_list = [2.0 * center * neighbour / (center + neighbour) for neighbour in others]
    diagonal = face_list[0]
    for weight in face_list[1:]:
        diagonal = diagonal + weight
    return (face_list, diagonal)

def stencil(field_pad, face_list, diagonal):
    slices = [field_pad[:, 2:, 1:-1, 1:-1], field_pad[:, :-2, 1:-1, 1:-1], field_pad[:, 1:-1, 2:, 1:-1], field_pad[:, 1:-1, :-2, 1:-1], field_pad[:, 1:-1, 1:-1, 2:], field_pad[:, 1:-1, 1:-1, :-2]]
    accum = face_list[0] * slices[0]
    for weight, piece in zip(face_list[1:], slices[1:]):
        accum = accum + weight * piece
    return 2.5 * accum / diagonal

def reference(right_sides, permeability):
    kappa_pad = jnp.pad(permeability, 1)
    face_list, diagonal = face_weights(kappa_pad)
    powers = [right_sides]
    field = right_sides
    for power_index in range(SSTEP):
        padded = jnp.pad(field, ((0, 0), (1, 1), (1, 1), (1, 1)))
        field = stencil(padded, face_list, diagonal)
        powers.append(field)
    basis = jnp.concatenate(powers, 0)
    flat = basis.reshape(NCOL, -1)
    gram = jnp.dot(flat, flat.T, precision=lax.Precision.HIGHEST)
    factor_r = jnp.linalg.cholesky(gram / CELLS).T
    solved = lax.linalg.triangular_solve(factor_r, flat, left_side=True, lower=False, transpose_a=True)
    return (solved.reshape(basis.shape), factor_r)
```

```python
import functools

import jax
import jax.numpy as jnp
from jax import lax
from jax.experimental import pallas as pl
from jax.experimental.pallas import tpu as pltpu
from jax.sharding import PartitionSpec as P

NF = 6
DEPTH = 3
LEVELS = DEPTH + 1
NC = NF * LEVELS
CH = 8
TILES = 4
ROWS = NC * 8
MESH = pl.DeviceIdType.MESH
F32 = jnp.float32
BF16 = jnp.bfloat16
HIGH = lax.Precision.HIGHEST


def iota(shape, dim):
    return lax.broadcasted_iota(jnp.int32, shape, dim)


def nt(left, right, precision=None):
    return lax.dot_general(
        left, right, (((1,), (1,)), ((), ())), precision=precision, preferred_element_type=F32
    )


def lane_roll(value, amount):
    return pltpu.roll(value, amount % 128, 1)


def shifted_rows(tiles, before, after, row):
    rolled = [pltpu.roll(v, 1, 0) for v in tiles]
    upper = [jnp.where(row == 0, p, r) for p, r in zip([before] + rolled[:-1], rolled)]
    rolled = [pltpu.roll(v, 7, 0) for v in tiles]
    lower = [jnp.where(row == 7, n, r) for n, r in zip(rolled[1:] + [after], rolled)]
    return upper, lower


def shifted_lanes(value, pair, lane):
    left = lane_roll(jnp.where(lane == 127, pair, value), 1)
    right = lane_roll(jnp.where(lane == 0, pair, value), 127)
    return left, right


def basis_kernel(
    sizes, cells, rs, kap, hl, wmat, factor,
    kp, kys, kyr, kzs, kzr, vv, aa, ys, yr, zs, zr, acc, msg, slot1, slot2,
    load_sem, ks_sem, kr_sem, xs_sem, xr_sem, ys_sem, yr_sem, zs_sem, zr_sem,
    s1_sem, r1_sem, s2_sem, r2_sem,
):
    gx, gy, gz = sizes
    nx = kp.shape[0] - 2
    chunks = nx // CH
    ix, iy, iz = lax.axis_index("gx"), lax.axis_index("gy"), lax.axis_index("gz")
    at = {"gx": ix, "gy": iy, "gz": iz}
    size = {"gx": gx, "gy": gy, "gz": gz}

    def toward(axis, by):
        return {axis: lax.rem(at[axis] + (by + size[axis]), size[axis])}

    kap_copy = pltpu.make_async_copy(kap, kp.at[pl.ds(1, nx)], load_sem.at[NF])
    kap_copy.start()
    field_copies = []
    for f in range(NF):
        copy = pltpu.make_async_copy(rs.at[f], vv.at[0, pl.ds(1, nx), f], load_sem.at[f])
        copy.start()
        field_copies.append(copy)

    n1 = gx * gy
    rank1 = ix * gy + iy
    group1 = []
    for d in range(1, n1):
        other = lax.rem(rank1 + d, n1)
        group1.append({"gx": other // gy, "gy": lax.rem(other, gy)})
    group2 = [{"gz": lax.rem(iz + d, gz)} for d in range(1, gz)]
    barrier = pltpu.get_barrier_semaphore()
    for device in group1 + group2:
        pl.semaphore_signal(barrier, inc=1, device_id=device, device_id_type=MESH)

    lane = iota((8, 128), 1)
    row = iota((8, 128), 0)
    even = (lane & 1) == 0
    zero = jnp.zeros((8, 128), F32)

    def remote(src, dst, send, recv, device):
        return pltpu.make_async_remote_copy(
            src_ref=src, dst_ref=dst, send_sem=send, recv_sem=recv,
            device_id=device, device_id_type=MESH,
        )

    kap_copy.wait()

    def pack_kap(x, carry):
        tiles = [kp[x + 1, t * 8:(t + 1) * 8, :] for t in range(TILES)]
        kys[0, pl.ds(x, 1), :] = tiles[0][0:1]
        kys[1, pl.ds(x, 1), :] = tiles[3][7:8]
        result = []
        for m in range(2):
            both = jnp.where(lane < 64, lane_roll(tiles[2 * m], 1), lane_roll(tiles[2 * m + 1], 65))
            both = pltpu.roll(both, 2 * x, 1)
            result.append(jnp.where(((lane >> 1) & 31) == x, both, carry[m]))
        return tuple(result)

    packed = lax.fori_loop(0, nx, pack_kap, (zero, zero))
    for m in range(2):
        kzs[m] = packed[m]
    pl.semaphore_wait(barrier, n1 - 1 + gz - 1)

    kap_sends = [
        remote(kp.at[nx], kp.at[0], ks_sem.at[0], kr_sem.at[0], toward("gx", 1)),
        remote(kp.at[1], kp.at[nx + 1], ks_sem.at[1], kr_sem.at[1], toward("gx", -1)),
        remote(kys.at[1], kyr.at[0], ks_sem.at[2], kr_sem.at[2], toward("gy", 1)),
        remote(kys.at[0], kyr.at[1], ks_sem.at[3], kr_sem.at[3], toward("gy", -1)),
        remote(kzs, kzr.at[0], ks_sem.at[4], kr_sem.at[4], toward("gz", 1)),
        remote(kzs, kzr.at[1], ks_sem.at[5], kr_sem.at[5], toward("gz", -1)),
    ]
    for copy in kap_sends:
        copy.start()

    def x_copy(level, side):
        src, dst = (nx, 0) if side == 0 else (1, nx + 1)
        return remote(
            vv.at[level, src], vv.at[level, dst], xs_sem.at[level, side], xr_sem.at[level, side],
            toward("gx", 1 - 2 * side),
        )

    def y_copy(level, side, c):
        part = pl.ds(pl.multiple_of(c * CH, CH), CH)
        return remote(
            ys.at[level, 1 - side, :, part, :], yr.at[level, side, :, part, :],
            ys_sem.at[level, side, c], yr_sem.at[level, side, c], toward("gy", 1 - 2 * side),
        )

    def z_copy(level, side, c):
        return remote(
            zs.at[level, c], zr.at[level, side, c],
            zs_sem.at[level, side, c], zr_sem.at[level, side, c], toward("gz", 1 - 2 * side),
        )

    def emit(level, x, i, fields, carry):
        for f in range(0, NF, 2):
            at_row = (level * NF + f) * 8
            for t in range(TILES):
                full = jnp.concatenate([fields[f][t], fields[f + 1][t]], 0)
                high = full.astype(BF16)
                low = (full - high.astype(F32)).astype(BF16)
                hl[x, 0, at_row:at_row + 16, t * 128:(t + 1) * 128] = high
                hl[x, 1, at_row:at_row + 16, t * 128:(t + 1) * 128] = low
        if level == DEPTH:
            return carry
        result = []
        for m in range(NF // 2):
            merged = None
            for g in range(2 * TILES):
                piece = lane_roll(fields[2 * m + g // TILES][g % TILES], 16 * g + 1)
                merged = piece if merged is None else jnp.where(lane < 16 * g, merged, piece)
            merged = pltpu.roll(merged, 2 * i, 1)
            result.append(jnp.where(((lane >> 1) & 7) == i, merged, carry[m]))
        for f in range(NF):
            ys[level, 0, f, pl.ds(x, 1), :] = fields[f][0][0:1]
            ys[level, 1, f, pl.ds(x, 1), :] = fields[f][TILES - 1][7:8]
        return tuple(result)

    def send_chunk(level, q, c, carry):
        for m in range(NF // 2):
            zs[level, c, m] = carry[m]
        for side in range(2):
            y_copy(level, side, c).start()
            z_copy(level, side, c).start()
        if level > 0:
            @pl.when(q == 0)
            def _():
                x_copy(level, 1).start()

            @pl.when(q == 1)
            def _():
                x_copy(level, 0).start()

    def tiles_of(level, plane, f):
        return [vv[level, plane, f, t * 8:(t + 1) * 8, :] for t in range(TILES)]

    def order(q):
        return lax.rem(q * (chunks - 1), chunks)

    for copy in field_copies:
        copy.wait()
    for side in range(2):
        x_copy(0, side).start()

    def first_chunk(q, nothing):
        c = order(q)

        def plane(i, carry):
            x = c * CH + i
            return emit(0, x, i, [tiles_of(0, x + 1, f) for f in range(NF)], carry)

        send_chunk(0, q, c, lax.fori_loop(0, CH, plane, (zero,) * 3))
        return nothing

    lax.fori_loop(0, chunks, first_chunk, 0)

    for copy in kap_sends:
        copy.wait_recv()

    def inside(axis, by):
        edge = 0 if by < 0 else size[axis] - 1
        return jnp.where(at[axis] == edge, 0.0, 1.0).astype(F32)

    def weights(x, nothing):
        own = [kp[x + 1, t * 8:(t + 1) * 8, :] for t in range(TILES)]
        x_low = jnp.where(x == 0, inside("gx", -1), 1.0)
        x_high = jnp.where(x == nx - 1, inside("gx", 1), 1.0)
        before = jnp.broadcast_to(kyr[0, pl.ds(x, 1), :] * inside("gy", -1), (8, 128))
        after = jnp.broadcast_to(kyr[1, pl.ds(x, 1), :] * inside("gy", 1), (8, 128))
        upper, lower = shifted_rows(own, before, after, row)
        turned = []
        for m in range(2):
            both = jnp.where(even, kzr[0, m] * inside("gz", -1), kzr[1, m] * inside("gz", 1))
            turned.append(pltpu.roll(both, lax.rem(128 - 2 * x, 128), 1))
        for t in range(TILES):
            pair = lane_roll(turned[t // 2], 127 - 64 * (t % 2))
            left, right = shifted_lanes(own[t], pair, lane)
            part = slice(t * 8, (t + 1) * 8)
            others = [
                kp[x + 2, part, :] * x_high, kp[x, part, :] * x_low,
                lower[t], upper[t], right, left,
            ]
            faces = [2.0 * own[t] * other / (own[t] + other) for other in others]
            diagonal = faces[0]
            for face in faces[1:]:
                diagonal = diagonal + face
            scale = 2.5 / diagonal
            for n in range(6):
                aa[x, n, part, :] = faces[n] * scale
        return nothing

    lax.fori_loop(0, nx, weights, 0)

    for level in range(DEPTH):
        def chunk(q, nothing, level=level):
            c = order(q)
            for side in range(2):
                y_copy(level, side, c).wait_recv()
                z_copy(level, side, c).wait_recv()

            @pl.when(q == 0)
            def _():
                x_copy(level, 0).wait_recv()

            @pl.when(q == 1)
            def _():
                x_copy(level, 1).wait_recv()

            def plane(i, carry):
                x = c * CH + i
                turned = []
                for m in range(NF // 2):
                    both = jnp.where(even, zr[level, 0, c, m], zr[level, 1, c, m])
                    turned.append(pltpu.roll(both, lax.rem(128 - 2 * i, 128), 1))
                fields = []
                for f in range(NF):
                    own = tiles_of(level, x + 1, f)
                    low = tiles_of(level, x, f)
                    high = tiles_of(level, x + 2, f)
                    before = jnp.broadcast_to(yr[level, 0, f, pl.ds(x, 1), :], (8, 128))
                    after = jnp.broadcast_to(yr[level, 1, f, pl.ds(x, 1), :], (8, 128))
                    upper, lower = shifted_rows(own, before, after, row)
                    tiles = []
                    for t in range(TILES):
                        g = (f % 2) * TILES + t
                        pair = lane_roll(turned[f // 2], 127 - 16 * g)
                        left, right = shifted_lanes(own[t], pair, lane)
                        part = slice(t * 8, (t + 1) * 8)
                        total = aa[x, 0, part, :] * high[t]
                        total = total + aa[x, 1, part, :] * low[t]
                        total = total + aa[x, 2, part, :] * lower[t]
                        total = total + aa[x, 3, part, :] * upper[t]
                        total = total + aa[x, 4, part, :] * right
                        total = total + aa[x, 5, part, :] * left
                        tiles.append(total)
                        if level + 1 < DEPTH:
                            vv[level + 1, x + 1, f, part, :] = total
                    fields.append(tiles)
                return emit(level + 1, x, i, fields, carry)

            carry = lax.fori_loop(0, CH, plane, (zero,) * 3)
            if level + 1 < DEPTH:
                send_chunk(level + 1, q, c, carry)
            return nothing

        lax.fori_loop(0, chunks, chunk, 0)

    acc[...] = jnp.zeros_like(acc)

    def products(x, nothing):
        acc[...] += nt(hl[x].reshape(2 * ROWS, TILES * 128), hl[x, 0])
        return nothing

    lax.fori_loop(0, nx, products, 0)

    same = (iota((ROWS, ROWS), 0) & 7) == (iota((ROWS, ROWS), 1) & 7)
    mixed = jnp.where(same, acc[0:ROWS] + 2.0 * acc[ROWS:], 0.0)
    pick_rows = ((iota((NC, ROWS), 1) >> 3) == iota((NC, ROWS), 0)).astype(F32)
    spread = ((iota((ROWS, 128), 0) >> 3) == iota((ROWS, 128), 1)).astype(F32)
    small = jnp.dot(pick_rows, mixed, precision=HIGH, preferred_element_type=F32)
    small = jnp.dot(small, spread, precision=HIGH, preferred_element_type=F32)
    message = small[0:8] + lane_roll(small[8:16], 32) + lane_roll(small[16:24], 64)

    msg[0] = message
    slot1[rank1] = message
    sends1 = []
    for d, device in enumerate(group1):
        copy = remote(msg.at[0], slot1.at[rank1], s1_sem.at[d], r1_sem.at[rank1], device)
        copy.start()
        sends1.append(copy)
    for d in range(1, n1):
        source = lax.rem(rank1 + d, n1)
        remote(msg.at[0], slot1.at[source], s1_sem.at[0], r1_sem.at[source], group1[0]).wait_recv()
    message = slot1[0]
    for d in range(1, n1):
        message = message + slot1[d]
    msg[1] = message
    slot2[iz] = message
    sends2 = []
    for d, device in enumerate(group2):
        copy = remote(msg.at[1], slot2.at[iz], s2_sem.at[d], r2_sem.at[iz], device)
        copy.start()
        sends2.append(copy)
    for d in range(1, gz):
        source = lax.rem(iz + d, gz)
        remote(msg.at[1], slot2.at[source], s2_sem.at[0], r2_sem.at[source], group2[0]).wait_recv()
    message = slot2[0]
    for d in range(1, gz):
        message = message + slot2[d]

    message = message * (0.5 / cells)
    lanes = iota((NC, 128), 1)
    rows = iota((NC, 128), 0)
    parts = [message, lane_roll(message, 96), lane_roll(message, 64)]
    half = jnp.where(lanes < NC, jnp.concatenate(parts, 0), 0.0)
    identity = (lanes == rows).astype(F32)
    padded = jnp.concatenate([half, jnp.zeros((128 - NC, 128), F32)], 0)
    matrix = half + nt(identity, padded, HIGH) + (lanes == rows + 32).astype(F32)
    pivots = jnp.ones((NC, 128), F32)
    for k in range(NC):
        pivot_row = jnp.broadcast_to(matrix[k:k + 1, :], (NC, 128))
        column = jnp.broadcast_to(matrix[:, k:k + 1], (NC, 128))
        pivot = jnp.broadcast_to(column[k:k + 1, :], (NC, 128))
        pivots = jnp.where(rows == k, pivot, pivots)
        factors = jnp.where(rows > k, column / pivot, 0.0)
        matrix = matrix - factors * pivot_row
    matrix = matrix * (1.0 / jnp.sqrt(pivots))
    factor[...] = jnp.where((lanes >= rows) & (lanes < NC), matrix, 0.0)
    inverse = jnp.where(lanes <= rows, lane_roll(matrix, 96), 0.0)

    padded = jnp.concatenate([inverse, jnp.zeros((128 - NC, 128), F32)], 0)
    high = padded.astype(BF16)
    low = (padded - high.astype(F32)).astype(BF16)
    spread = spread.astype(BF16)
    for which, piece in enumerate((high, low)):
        wide = jnp.dot(spread, piece, preferred_element_type=F32).astype(BF16)
        wide = jnp.where(same, nt(wide, spread), 0.0).astype(BF16)
        wmat[which] = wide

    for copy in kap_sends + sends1 + sends2:
        copy.wait_send()
    for level in range(DEPTH):
        for side in range(2):
            x_copy(level, side).wait_send()

            def drain(c, nothing, level=level, side=side):
                y_copy(level, side, c).wait_send()
                z_copy(level, side, c).wait_send()
                return nothing

            lax.fori_loop(0, chunks, drain, 0)


def solve_kernel(wmat, factor, hl, q, r):
    x = pl.program_id(0)
    high, low = hl[x, 0], hl[x, 1]
    weights = jnp.concatenate([wmat[0], wmat[0], wmat[1]], 1)
    result = jnp.dot(weights, jnp.concatenate([high, low, high], 0), preferred_element_type=F32)
    for f in range(NC):
        for t in range(TILES):
            q[f, 0, t * 8:(t + 1) * 8, :] = result[f * 8:(f + 1) * 8, t * 128:(t + 1) * 128]

    @pl.when(x == 0)
    def _():
        r[...] = factor[:, 0:NC]


def on_device(sizes, right_sides, permeability):
    nx, ny, nz = permeability.shape
    chunks = nx // CH
    cells = float(nx * ny * nz * sizes[0] * sizes[1] * sizes[2])
    n1, n2 = sizes[0] * sizes[1], sizes[2]
    dma = pltpu.SemaphoreType.DMA
    vmem = pl.BlockSpec(memory_space=pltpu.VMEM)
    hl, wmat, factor = pl.pallas_call(
        functools.partial(basis_kernel, sizes, cells),
        out_shape=(
            pltpu.VMEM((nx, 2, ROWS, TILES * 128), BF16),
            pltpu.VMEM((2, ROWS, ROWS), BF16),
            pltpu.VMEM((NC, 128), F32),
        ),
        in_specs=[pl.BlockSpec(memory_space=pl.ANY)] * 2,
        out_specs=(vmem, vmem, vmem),
        scratch_shapes=[
            pltpu.VMEM((nx + 2, ny, 128), F32),
            pltpu.VMEM((2, nx, 128), F32),
            pltpu.VMEM((2, nx, 128), F32),
            pltpu.VMEM((2, 8, 128), F32),
            pltpu.VMEM((2, 2, 8, 128), F32),
            pltpu.VMEM((DEPTH, nx + 2, NF, ny, 128), F32),
            pltpu.VMEM((nx, 6, ny, 128), F32),
            pltpu.VMEM((DEPTH, 2, NF, nx, 128), F32),
            pltpu.VMEM((DEPTH, 2, NF, nx, 128), F32),
            pltpu.VMEM((DEPTH, chunks, NF // 2, 8, 128), F32),
            pltpu.VMEM((DEPTH, 2, chunks, NF // 2, 8, 128), F32),
            pltpu.VMEM((2 * ROWS, ROWS), F32),
            pltpu.VMEM((2, 8, 128), F32),
            pltpu.VMEM((n1, 8, 128), F32),
            pltpu.VMEM((n2, 8, 128), F32),
            dma((NF + 1,)),
            dma((6,)), dma((6,)),
            dma((DEPTH, 2)), dma((DEPTH, 2)),
            dma((DEPTH, 2, chunks)), dma((DEPTH, 2, chunks)),
            dma((DEPTH, 2, chunks)), dma((DEPTH, 2, chunks)),
            dma((n1 - 1,)), dma((n1,)),
            dma((n2 - 1,)), dma((n2,)),
        ],
        compiler_params=pltpu.CompilerParams(
            collective_id=0, has_side_effects=True, vmem_limit_bytes=44 * 1024 * 1024
        ),
        name="basis",
    )(right_sides, permeability)
    return pl.pallas_call(
        solve_kernel,
        grid=(nx,),
        out_shape=(
            jax.ShapeDtypeStruct((NC, nx, ny, 128), F32),
            jax.ShapeDtypeStruct((NC, NC), F32),
        ),
        in_specs=[vmem, vmem, vmem],
        out_specs=(
            pl.BlockSpec((NC, 1, ny, 128), lambda x: (0, x, 0, 0)),
            pl.BlockSpec((NC, NC), lambda x: (0, 0)),
        ),
        compiler_params=pltpu.CompilerParams(vmem_limit_bytes=8 * 1024 * 1024),
        name="solve",
    )(wmat, factor, hl)


def solution(mesh):
    sizes = tuple(mesh.shape[axis] for axis in ("gx", "gy", "gz"))
    return jax.shard_map(
        functools.partial(on_device, sizes),
        mesh=mesh,
        in_specs=(P(None, "gx", "gy", "gz"), P("gx", "gy", "gz")),
        out_specs=(P(None, "gx", "gy", "gz"), P()),
        check_vma=False,
    )
```

```python
import functools

import jax
import jax.numpy as jnp
from jax import lax
from jax.experimental import pallas as pl
from jax.experimental.pallas import tpu as pltpu
from jax.sharding import PartitionSpec as P

NF = 6
DEPTH = 3
LEVELS = DEPTH + 1
NC = NF * LEVELS
CH = 8
TILES = 4
ROWS = NC * 8
BAND = NF * 8
UNIT = 4
GROUP = 8
SPAN = 4
SLOTS = 4
MESH = pl.DeviceIdType.MESH
F32 = jnp.float32
BF16 = jnp.bfloat16
HIGH = lax.Precision.HIGHEST


def iota(shape, dim):
    return lax.broadcasted_iota(jnp.int32, shape, dim)


def nt(left, right, precision=None):
    return lax.dot_general(
        left, right, (((1,), (1,)), ((), ())), precision=precision, preferred_element_type=F32
    )


def reciprocal(value):
    guess = pl.reciprocal(value, approx=True)
    return guess * (2.0 - value * guess)


def lane_roll(value, amount):
    return pltpu.roll(value, amount % 128, 1)


def shifted_rows(tiles, before, after, row):
    rolled = [pltpu.roll(v, 1, 0) for v in tiles]
    upper = [jnp.where(row == 0, p, r) for p, r in zip([before] + rolled[:-1], rolled)]
    rolled = [pltpu.roll(v, 7, 0) for v in tiles]
    lower = [jnp.where(row == 7, n, r) for n, r in zip(rolled[1:] + [after], rolled)]
    return upper, lower


def shifted_lanes(value, pair, lane):
    left = lane_roll(jnp.where(lane == 127, pair, value), 1)
    right = lane_roll(jnp.where(lane == 0, pair, value), 127)
    return left, right


def basis_kernel(
    sizes, cells, rs, kap, hl0, hl1, hl2, hl3, wmat, factor,
    kp, kys, kyr, kzs, kzr, v0, v1, v2, aa, ys, yr, zs, zr, shift, gather, acc, msg, slot1, slot2,
    load_sem, ks_sem, kr_sem, xs_sem, xr_sem, ys_sem, yr_sem, zs_sem, zr_sem,
    s1_sem, r1_sem, s2_sem, r2_sem,
):
    hl = (hl0, hl1, hl2, hl3)
    vv = (v0, v1, v2)
    gx, gy, gz = sizes
    nx = kp.shape[0] - 2
    chunks = nx // CH
    ix, iy, iz = lax.axis_index("gx"), lax.axis_index("gy"), lax.axis_index("gz")
    at = {"gx": ix, "gy": iy, "gz": iz}
    size = {"gx": gx, "gy": gy, "gz": gz}

    def toward(axis, by):
        return {axis: lax.rem(at[axis] + (by + size[axis]), size[axis])}

    kap_copy = pltpu.make_async_copy(kap, kp.at[pl.ds(1, nx)], load_sem.at[NF])
    kap_copy.start()
    field_copies = []
    for f in range(NF):
        copy = pltpu.make_async_copy(rs.at[f], v0.at[pl.ds(1, nx), f], load_sem.at[f])
        copy.start()
        field_copies.append(copy)

    n1 = gx * gy
    rank1 = ix * gy + iy
    group1 = []
    for d in range(1, n1):
        other = lax.rem(rank1 + d, n1)
        group1.append({"gx": other // gy, "gy": lax.rem(other, gy)})
    group2 = [{"gz": lax.rem(iz + d, gz)} for d in range(1, gz)]
    barrier = pltpu.get_barrier_semaphore()
    for device in group1 + group2:
        pl.semaphore_signal(barrier, inc=1, device_id=device, device_id_type=MESH)

    lane = iota((8, 128), 1)
    row = iota((8, 128), 0)
    even = (lane & 1) == 0
    zero = jnp.zeros((8, 128), F32)

    def remote(src, dst, send, recv, device):
        return pltpu.make_async_remote_copy(
            src_ref=src, dst_ref=dst, send_sem=send, recv_sem=recv,
            device_id=device, device_id_type=MESH,
        )

    source, target = iota((256, 256), 0) & 127, iota((256, 256), 1)
    wanted = jnp.where(target < 128, target - 1, target - 127)
    shift[0:256] = (source == wanted).astype(F32).astype(BF16)
    wanted = jnp.where((source & 1) == 0, 0, 255)
    shift[256:512] = (target == wanted).astype(F32).astype(BF16)
    source, target = iota((256, 128), 0) & 127, iota((256, 128), 1)
    wanted = jnp.where((target & 1) == 0, 127, 0)
    gather[...] = (source == wanted).astype(F32).astype(BF16)

    kap_copy.wait()

    def pack_kap(x, carry):
        tiles = [kp[x + 1, t * 8:(t + 1) * 8, :] for t in range(TILES)]
        kys[0, pl.ds(x, 1), :] = tiles[0][0:1]
        kys[1, pl.ds(x, 1), :] = tiles[3][7:8]
        result = []
        for m in range(2):
            both = jnp.where(lane < 64, lane_roll(tiles[2 * m], 1), lane_roll(tiles[2 * m + 1], 65))
            both = pltpu.roll(both, 2 * x, 1)
            result.append(jnp.where(((lane >> 1) & 31) == x, both, carry[m]))
        return tuple(result)

    packed = lax.fori_loop(0, nx, pack_kap, (zero, zero), unroll=8)
    for m in range(2):
        kzs[m] = packed[m]
    pl.semaphore_wait(barrier, n1 - 1 + gz - 1)

    kap_sends = [
        remote(kp.at[nx], kp.at[0], ks_sem.at[0], kr_sem.at[0], toward("gx", 1)),
        remote(kp.at[1], kp.at[nx + 1], ks_sem.at[1], kr_sem.at[1], toward("gx", -1)),
        remote(kys.at[1], kyr.at[0], ks_sem.at[2], kr_sem.at[2], toward("gy", 1)),
        remote(kys.at[0], kyr.at[1], ks_sem.at[3], kr_sem.at[3], toward("gy", -1)),
        remote(kzs, kzr.at[0], ks_sem.at[4], kr_sem.at[4], toward("gz", 1)),
        remote(kzs, kzr.at[1], ks_sem.at[5], kr_sem.at[5], toward("gz", -1)),
    ]
    for copy in kap_sends:
        copy.start()

    def x_copy(level, side):
        src, dst = (nx, 0) if side == 0 else (1, nx + 1)
        return remote(
            vv[level].at[src], vv[level].at[dst], xs_sem.at[level, side], xr_sem.at[level, side],
            toward("gx", 1 - 2 * side),
        )

    def y_copy(level, side, c):
        part = pl.ds(pl.multiple_of(c * CH, CH), CH)
        return remote(
            ys.at[level, 1 - side, :, part, :], yr.at[level, side, :, part, :],
            ys_sem.at[level, side, c], yr_sem.at[level, side, c], toward("gy", 1 - 2 * side),
        )

    def z_copy(level, side, c):
        return remote(
            zs.at[level, c], zr.at[level, side, c],
            zs_sem.at[level, side, c], zr_sem.at[level, side, c], toward("gz", 1 - 2 * side),
        )

    def emit(level, x, fields):
        for f in range(0, NF, 2):
            for t in range(TILES):
                full = jnp.concatenate([fields[f][t], fields[f + 1][t]], 0)
                high = full.astype(BF16)
                low = (full - high.astype(F32)).astype(BF16)
                hl[level][x, 0, f * 8:f * 8 + 16, t * 128:(t + 1) * 128] = high
                hl[level][x, 1, f * 8:f * 8 + 16, t * 128:(t + 1) * 128] = low
        if level < DEPTH:
            for f in range(NF):
                ys[level, 0, f, pl.ds(x, 1), :] = fields[f][0][0:1]
                ys[level, 1, f, pl.ds(x, 1), :] = fields[f][TILES - 1][7:8]

    def halves(level, x, count, t):
        part = slice(t * 128, (t + 1) * 128)
        return jnp.concatenate(
            [hl[level][pl.ds(x, count), h, :, part].reshape(count * BAND, 128) for h in range(2)], 1
        )

    def pack_chunk(level, c):
        result = [zero] * (NF // 2)
        for t in range(TILES):
            outer = jnp.dot(
                halves(level, c * CH, CH, t), gather[...], preferred_element_type=F32
            )
            for i in range(CH):
                for f in range(NF):
                    at_row = (i * NF + f) * 8
                    mask = (lane >> 1) == ((f % 2) * TILES + t) * CH + i
                    result[f // 2] = jnp.where(mask, outer[at_row:at_row + 8], result[f // 2])
        for m in range(NF // 2):
            zs[level, c, m] = result[m]

    def send_chunk(level, q, c):
        for side in range(2):
            y_copy(level, side, c).start()
        if level > 0:
            @pl.when(q == 0)
            def _():
                x_copy(level, 1).start()

            @pl.when(q == 1)
            def _():
                x_copy(level, 0).start()

        pack_chunk(level, c)
        for side in range(2):
            z_copy(level, side, c).start()

    def tiles_of(level, plane, f):
        return [vv[level][plane, f, t * 8:(t + 1) * 8, :] for t in range(TILES)]

    def order(q):
        return lax.rem(q * (chunks - 1), chunks)

    for copy in field_copies:
        copy.wait()
    for side in range(2):
        x_copy(0, side).start()

    def first_chunk(q, nothing):
        c = order(q)

        def plane(i, nothing):
            x = c * CH + i
            emit(0, x, [tiles_of(0, x + 1, f) for f in range(NF)])
            return nothing

        lax.fori_loop(0, CH, plane, 0, unroll=2)
        send_chunk(0, q, c)
        return nothing

    lax.fori_loop(0, chunks, first_chunk, 0)

    for copy in kap_sends:
        copy.wait_recv()

    def inside(axis, by):
        edge = 0 if by < 0 else size[axis] - 1
        return jnp.where(at[axis] == edge, 0.0, 1.0).astype(F32)

    def weights(x, nothing):
        own = [kp[x + 1, t * 8:(t + 1) * 8, :] for t in range(TILES)]
        x_low = jnp.where(x == 0, inside("gx", -1), 1.0)
        x_high = jnp.where(x == nx - 1, inside("gx", 1), 1.0)
        before = jnp.broadcast_to(kyr[0, pl.ds(x, 1), :] * inside("gy", -1), (8, 128))
        after = jnp.broadcast_to(kyr[1, pl.ds(x, 1), :] * inside("gy", 1), (8, 128))
        upper, lower = shifted_rows(own, before, after, row)
        turned = []
        for m in range(2):
            both = jnp.where(even, kzr[0, m] * inside("gz", -1), kzr[1, m] * inside("gz", 1))
            turned.append(pltpu.roll(both, lax.rem(128 - 2 * x, 128), 1))
        for t in range(TILES):
            pair = lane_roll(turned[t // 2], 127 - 64 * (t % 2))
            left, right = shifted_lanes(own[t], pair, lane)
            part = slice(t * 8, (t + 1) * 8)
            others = [
                kp[x + 2, part, :] * x_high, kp[x, part, :] * x_low,
                lower[t], upper[t], right, left,
            ]
            faces = [2.0 * own[t] * other * reciprocal(own[t] + other) for other in others]
            diagonal = faces[0]
            for face in faces[1:]:
                diagonal = diagonal + face
            scale = 2.5 * reciprocal(diagonal)
            for n in range(6):
                aa[x, n, part, :] = faces[n] * scale
        return nothing

    lax.fori_loop(0, nx, weights, 0, unroll=2)

    wide_lane = iota((16, 128), 1)
    second = jnp.where(iota((16, 128), 0) < 8, 0, TILES)
    groups = [((wide_lane >> 4) == second + t).astype(F32) for t in range(TILES)]

    for level in range(DEPTH):
        def chunk(q, nothing, level=level):
            c = order(q)
            for side in range(2):
                y_copy(level, side, c).wait_recv()
                z_copy(level, side, c).wait_recv()

            @pl.when(q == 0)
            def _():
                x_copy(level, 0).wait_recv()

            @pl.when(q == 1)
            def _():
                x_copy(level, 1).wait_recv()

            columns = [[], []]
            for m in range(NF // 2):
                both = jnp.where(even, zr[level, 0, c, m], zr[level, 1, c, m])
                high = both.astype(BF16)
                low = (both - high.astype(F32)).astype(BF16)
                columns[0].append(jnp.concatenate([high, high], 0))
                columns[1].append(jnp.concatenate([low, low], 0))

            def unit(u, nothing):
                x0 = c * CH + u * UNIT
                masks = []
                for i in range(UNIT):
                    mine = ((wide_lane >> 1) & (CH - 1)) == u * UNIT + i
                    masks.append([jnp.where(mine, g, 0.0).astype(BF16) for g in groups])
                left_part = []
                for t in range(TILES):
                    outer = [
                        jnp.concatenate(
                            [columns[h][m] * masks[i][t] for i in range(UNIT) for m in range(NF // 2)], 0
                        )
                        for h in range(2)
                    ]
                    left_part.append(jnp.concatenate([halves(level, x0, UNIT, t)] + outer, 1))
                moved = jnp.dot(
                    jnp.concatenate(left_part, 0), shift[...], preferred_element_type=F32
                )
                for i in range(UNIT):
                    x = x0 + i
                    fields = []
                    for f in range(NF):
                        own = tiles_of(level, x + 1, f)
                        low = tiles_of(level, x, f)
                        high = tiles_of(level, x + 2, f)
                        before = jnp.broadcast_to(yr[level, 0, f, pl.ds(x, 1), :], (8, 128))
                        after = jnp.broadcast_to(yr[level, 1, f, pl.ds(x, 1), :], (8, 128))
                        upper, lower = shifted_rows(own, before, after, row)
                        tiles = []
                        for t in range(TILES):
                            at_row = ((t * UNIT + i) * NF + f) * 8
                            part = slice(t * 8, (t + 1) * 8)
                            total = aa[x, 0, part, :] * high[t]
                            total = total + aa[x, 1, part, :] * low[t]
                            total = total + aa[x, 2, part, :] * lower[t]
                            total = total + aa[x, 3, part, :] * upper[t]
                            total = total + aa[x, 4, part, :] * moved[at_row:at_row + 8, 128:]
                            total = total + aa[x, 5, part, :] * moved[at_row:at_row + 8, :128]
                            tiles.append(total)
                            if level + 1 < DEPTH:
                                vv[level + 1][x + 1, f, part, :] = total
                        fields.append(tiles)
                    emit(level + 1, x, fields)
                return nothing

            lax.fori_loop(0, CH // UNIT, unit, 0)
            if level + 1 < DEPTH:
                send_chunk(level + 1, q, c)
            return nothing

        lax.fori_loop(0, chunks, chunk, 0)

    acc[...] = jnp.zeros_like(acc)

    def products(g, nothing):
        high, low = [
            jnp.concatenate(
                [
                    jnp.concatenate([ref[g * GROUP + i, h] for ref in hl], 0)
                    for i in range(GROUP)
                ],
                1,
            )
            for h in range(2)
        ]
        acc[...] += nt(jnp.concatenate([high, low], 0), high)
        return nothing

    lax.fori_loop(0, nx // GROUP, products, 0)

    same = (iota((ROWS, ROWS), 0) & 7) == (iota((ROWS, ROWS), 1) & 7)
    mixed = jnp.where(same, acc[0:ROWS] + 2.0 * acc[ROWS:], 0.0)
    pick_rows = ((iota((NC, ROWS), 1) >> 3) == iota((NC, ROWS), 0)).astype(F32)
    spread = ((iota((ROWS, 128), 0) >> 3) == iota((ROWS, 128), 1)).astype(F32)
    small = jnp.dot(pick_rows, mixed, precision=HIGH, preferred_element_type=F32)
    small = jnp.dot(small, spread, precision=HIGH, preferred_element_type=F32)
    message = small[0:8] + lane_roll(small[8:16], 32) + lane_roll(small[16:24], 64)

    msg[0] = message
    slot1[rank1] = message
    sends1 = []
    for d, device in enumerate(group1):
        copy = remote(msg.at[0], slot1.at[rank1], s1_sem.at[d], r1_sem.at[rank1], device)
        copy.start()
        sends1.append(copy)
    for d in range(1, n1):
        source = lax.rem(rank1 + d, n1)
        remote(msg.at[0], slot1.at[source], s1_sem.at[0], r1_sem.at[source], group1[0]).wait_recv()
    message = slot1[0]
    for d in range(1, n1):
        message = message + slot1[d]
    msg[1] = message
    slot2[iz] = message
    sends2 = []
    for d, device in enumerate(group2):
        copy = remote(msg.at[1], slot2.at[iz], s2_sem.at[d], r2_sem.at[iz], device)
        copy.start()
        sends2.append(copy)
    for d in range(1, gz):
        source = lax.rem(iz + d, gz)
        remote(msg.at[1], slot2.at[source], s2_sem.at[0], r2_sem.at[source], group2[0]).wait_recv()
    message = slot2[0]
    for d in range(1, gz):
        message = message + slot2[d]

    message = message * (0.5 / cells)
    lanes = iota((NC, 128), 1)
    rows = iota((NC, 128), 0)
    parts = [message, lane_roll(message, 96), lane_roll(message, 64)]
    half = jnp.where(lanes < NC, jnp.concatenate(parts, 0), 0.0)
    identity = (lanes == rows).astype(F32)
    padded = jnp.concatenate([half, jnp.zeros((128 - NC, 128), F32)], 0)
    matrix = half + nt(identity, padded, HIGH) + (lanes == rows + 32).astype(F32)
    pivots = jnp.ones((NC, 128), F32)
    for k in range(NC):
        pivot_row = jnp.broadcast_to(matrix[k:k + 1, :], (NC, 128))
        column = jnp.broadcast_to(matrix[:, k:k + 1], (NC, 128))
        pivot = jnp.broadcast_to(column[k:k + 1, :], (NC, 128))
        pivots = jnp.where(rows == k, pivot, pivots)
        factors = jnp.where(rows > k, column / pivot, 0.0)
        matrix = matrix - factors * pivot_row
    matrix = matrix * (1.0 / jnp.sqrt(pivots))
    factor[...] = jnp.where((lanes >= rows) & (lanes < NC), matrix, 0.0)
    inverse = jnp.where(lanes <= rows, lane_roll(matrix, 96), 0.0)

    padded = jnp.concatenate([inverse, jnp.zeros((128 - NC, 128), F32)], 0)
    high = padded.astype(BF16)
    low = (padded - high.astype(F32)).astype(BF16)
    spread = spread.astype(BF16)
    for which, piece in enumerate((high, low)):
        wide = jnp.dot(spread, piece, preferred_element_type=F32).astype(BF16)
        wide = jnp.where(same, nt(wide, spread), 0.0).astype(BF16)
        wmat[which] = wide

    for copy in kap_sends + sends1 + sends2:
        copy.wait_send()
    for level in range(DEPTH):
        for side in range(2):
            x_copy(level, side).wait_send()

            def drain(c, nothing, level=level, side=side):
                y_copy(level, side, c).wait_send()
                z_copy(level, side, c).wait_send()
                return nothing

            lax.fori_loop(0, chunks, drain, 0)


def solve_kernel(wmat, factor, hl0, hl1, hl2, hl3, q, r, held, sems):
    nx = hl0.shape[0]
    r[...] = factor[:, 0:NC]

    steps = nx // SPAN

    def out_copy(g):
        slot = lax.rem(g, SLOTS)
        return pltpu.make_async_copy(held.at[slot], q.at[:, pl.ds(g * SPAN, SPAN)], sems.at[slot])

    def planes(g, nothing):
        @pl.when(g >= SLOTS)
        def _():
            out_copy(g - SLOTS).wait()

        slot = lax.rem(g, SLOTS)
        high, low = [
            jnp.concatenate(
                [
                    jnp.concatenate([ref[g * SPAN + i, h] for ref in (hl0, hl1, hl2, hl3)], 0)
                    for i in range(SPAN)
                ],
                1,
            )
            for h in range(2)
        ]
        result = jnp.dot(wmat[0], high, preferred_element_type=F32)
        result = result + jnp.dot(wmat[0], low, preferred_element_type=F32)
        result = result + jnp.dot(wmat[1], high, preferred_element_type=F32)
        for f in range(NC):
            for i in range(SPAN):
                for t in range(TILES):
                    col = (i * TILES + t) * 128
                    held[slot, f, i, t * 8:(t + 1) * 8, :] = result[f * 8:(f + 1) * 8, col:col + 128]
        out_copy(g).start()
        return nothing

    lax.fori_loop(0, steps, planes, 0)

    def drain(g, nothing):
        out_copy(g).wait()
        return nothing

    lax.fori_loop(max(steps - SLOTS, 0), steps, drain, 0)


def on_device(sizes, right_sides, permeability):
    nx, ny, nz = permeability.shape
    chunks = nx // CH
    cells = float(nx * ny * nz * sizes[0] * sizes[1] * sizes[2])
    n1, n2 = sizes[0] * sizes[1], sizes[2]
    dma = pltpu.SemaphoreType.DMA
    vmem = pl.BlockSpec(memory_space=pltpu.VMEM)
    *hl, wmat, factor = pl.pallas_call(
        functools.partial(basis_kernel, sizes, cells),
        out_shape=(
            *[pltpu.VMEM((nx, 2, BAND, TILES * 128), BF16)] * LEVELS,
            pltpu.VMEM((2, ROWS, ROWS), BF16),
            pltpu.VMEM((NC, 128), F32),
        ),
        in_specs=[pl.BlockSpec(memory_space=pl.ANY)] * 2,
        out_specs=(vmem,) * (LEVELS + 2),
        scratch_shapes=[
            pltpu.VMEM((nx + 2, ny, 128), F32),
            pltpu.VMEM((2, nx, 128), F32),
            pltpu.VMEM((2, nx, 128), F32),
            pltpu.VMEM((2, 8, 128), F32),
            pltpu.VMEM((2, 2, 8, 128), F32),
            *[pltpu.VMEM((nx + 2, NF, ny, 128), F32)] * DEPTH,
            pltpu.VMEM((nx, 6, ny, 128), F32),
            pltpu.VMEM((DEPTH, 2, NF, nx, 128), F32),
            pltpu.VMEM((DEPTH, 2, NF, nx, 128), F32),
            pltpu.VMEM((DEPTH, chunks, NF // 2, 8, 128), F32),
            pltpu.VMEM((DEPTH, 2, chunks, NF // 2, 8, 128), F32),
            pltpu.VMEM((512, 256), BF16),
            pltpu.VMEM((256, 128), BF16),
            pltpu.VMEM((2 * ROWS, ROWS), F32),
            pltpu.VMEM((2, 8, 128), F32),
            pltpu.VMEM((n1, 8, 128), F32),
            pltpu.VMEM((n2, 8, 128), F32),
            dma((NF + 1,)),
            dma((6,)), dma((6,)),
            dma((DEPTH, 2)), dma((DEPTH, 2)),
            dma((DEPTH, 2, chunks)), dma((DEPTH, 2, chunks)),
            dma((DEPTH, 2, chunks)), dma((DEPTH, 2, chunks)),
            dma((n1 - 1,)), dma((n1,)),
            dma((n2 - 1,)), dma((n2,)),
        ],
        compiler_params=pltpu.CompilerParams(
            collective_id=0, has_side_effects=True, vmem_limit_bytes=44 * 1024 * 1024
        ),
        name="basis",
    )(right_sides, permeability)
    return pl.pallas_call(
        solve_kernel,
        out_shape=(
            jax.ShapeDtypeStruct((NC, nx, ny, 128), F32),
            jax.ShapeDtypeStruct((NC, NC), F32),
        ),
        in_specs=[vmem] * (LEVELS + 2),
        out_specs=(pl.BlockSpec(memory_space=pl.ANY), vmem),
        scratch_shapes=[
            pltpu.VMEM((SLOTS, NC, SPAN, ny, 128), F32),
            dma((SLOTS,)),
        ],
        compiler_params=pltpu.CompilerParams(vmem_limit_bytes=12 * 1024 * 1024),
        name="solve",
    )(wmat, factor, *hl)


def solution(mesh):
    sizes = tuple(mesh.shape[axis] for axis in ("gx", "gy", "gz"))
    return jax.shard_map(
        functools.partial(on_device, sizes),
        mesh=mesh,
        in_specs=(P(None, "gx", "gy", "gz"), P("gx", "gy", "gz")),
        out_specs=(P(None, "gx", "gy", "gz"), P()),
        check_vma=False,
    )
```

```python
import functools

import jax
import jax.numpy as jnp
from jax import lax
from jax.experimental import pallas as pl
from jax.experimental.pallas import tpu as pltpu
from jax.sharding import PartitionSpec as P

NF = 6
DEPTH = 3
LEVELS = DEPTH + 1
NC = NF * LEVELS
CH = 8
TILES = 4
ROWS = NC * 8
BAND = NF * 8
UNIT = 4
GROUP = 8
SPAN = 4
SLOTS = 4
MESH = pl.DeviceIdType.MESH
F32 = jnp.float32
BF16 = jnp.bfloat16
HIGH = lax.Precision.HIGHEST


def iota(shape, dim):
    return lax.broadcasted_iota(jnp.int32, shape, dim)


def nt(left, right, precision=None):
    return lax.dot_general(
        left, right, (((1,), (1,)), ((), ())), precision=precision, preferred_element_type=F32
    )


def reciprocal(value):
    guess = pl.reciprocal(value, approx=True)
    return guess * (2.0 - value * guess)


def lane_roll(value, amount):
    return pltpu.roll(value, amount % 128, 1)


def shifted_rows(tiles, before, after, row):
    rolled = [pltpu.roll(v, 1, 0) for v in tiles]
    upper = [jnp.where(row == 0, p, r) for p, r in zip([before] + rolled[:-1], rolled)]
    rolled = [pltpu.roll(v, 7, 0) for v in tiles]
    lower = [jnp.where(row == 7, n, r) for n, r in zip(rolled[1:] + [after], rolled)]
    return upper, lower


def shifted_lanes(value, pair, lane):
    left = lane_roll(jnp.where(lane == 127, pair, value), 1)
    right = lane_roll(jnp.where(lane == 0, pair, value), 127)
    return left, right


def basis_kernel(
    sizes, cells, rs, kap, hl0, hl1, hl2, hl3, wmat, factor,
    kp, kys, kyr, kzs, kzr, v0, v1, v2, aa, ys, yr, zs, zr, shift, gather, acc, msg, slot,
    load_sem, ks_sem, kr_sem, xs_sem, xr_sem, ys_sem, yr_sem, zs_sem, zr_sem,
    s_sem, r_sem,
):
    hl = (hl0, hl1, hl2, hl3)
    vv = (v0, v1, v2)
    gx, gy, gz = sizes
    nx, ny = kp.shape[0] - 2, kp.shape[1]
    chunks = nx // CH
    ix, iy, iz = lax.axis_index("gx"), lax.axis_index("gy"), lax.axis_index("gz")
    at = {"gx": ix, "gy": iy, "gz": iz}
    size = {"gx": gx, "gy": gy, "gz": gz}

    def toward(axis, by):
        return {axis: lax.rem(at[axis] + (by + size[axis]), size[axis])}

    kap_copy = pltpu.make_async_copy(kap, kp.at[pl.ds(1, nx)], load_sem.at[NF])
    kap_copy.start()
    field_copies = []
    for f in range(NF):
        copy = pltpu.make_async_copy(rs.at[f], v0.at[pl.ds(1, nx), f, pl.ds(8, ny)], load_sem.at[f])
        copy.start()
        field_copies.append(copy)

    n1 = gx * gy
    rank1 = ix * gy + iy
    barrier = pltpu.get_barrier_semaphore()
    greeted = []
    for d in range(1, n1):
        other = lax.rem(rank1 + d, n1)
        greeted.append({"gx": other // gy, "gy": lax.rem(other, gy)})
    greeted += [{"gz": lax.rem(iz + d, gz)} for d in range(1, gz)]
    for device in greeted:
        pl.semaphore_signal(barrier, inc=1, device_id=device, device_id_type=MESH)

    lane = iota((8, 128), 1)
    row = iota((8, 128), 0)
    even = (lane & 1) == 0
    zero = jnp.zeros((8, 128), F32)

    def remote(src, dst, send, recv, device):
        return pltpu.make_async_remote_copy(
            src_ref=src, dst_ref=dst, send_sem=send, recv_sem=recv,
            device_id=device, device_id_type=MESH,
        )

    source, target = iota((256, 256), 0) & 127, iota((256, 256), 1)
    wanted = jnp.where(target < 128, target - 1, target - 127)
    shift[0:256] = (source == wanted).astype(F32).astype(BF16)
    wanted = jnp.where((source & 1) == 0, 0, 255)
    shift[256:512] = (target == wanted).astype(F32).astype(BF16)
    source, target = iota((256, 128), 0) & 127, iota((256, 128), 1)
    wanted = jnp.where((target & 1) == 0, 127, 0)
    gather[...] = (source == wanted).astype(F32).astype(BF16)

    kap_copy.wait()

    def pack_kap(x, carry):
        tiles = [kp[x + 1, t * 8:(t + 1) * 8, :] for t in range(TILES)]
        kys[0, pl.ds(x, 1), :] = tiles[0][0:1]
        kys[1, pl.ds(x, 1), :] = tiles[3][7:8]
        result = []
        for m in range(2):
            both = jnp.where(lane < 64, lane_roll(tiles[2 * m], 1), lane_roll(tiles[2 * m + 1], 65))
            both = pltpu.roll(both, 2 * x, 1)
            result.append(jnp.where(((lane >> 1) & 31) == x, both, carry[m]))
        return tuple(result)

    packed = lax.fori_loop(0, nx, pack_kap, (zero, zero), unroll=8)
    for m in range(2):
        kzs[m] = packed[m]
    pl.semaphore_wait(barrier, n1 + gz - 2)

    kap_sends = [
        remote(kp.at[nx], kp.at[0], ks_sem.at[0], kr_sem.at[0], toward("gx", 1)),
        remote(kp.at[1], kp.at[nx + 1], ks_sem.at[1], kr_sem.at[1], toward("gx", -1)),
        remote(kys.at[1], kyr.at[0], ks_sem.at[2], kr_sem.at[2], toward("gy", 1)),
        remote(kys.at[0], kyr.at[1], ks_sem.at[3], kr_sem.at[3], toward("gy", -1)),
        remote(kzs, kzr.at[0], ks_sem.at[4], kr_sem.at[4], toward("gz", 1)),
        remote(kzs, kzr.at[1], ks_sem.at[5], kr_sem.at[5], toward("gz", -1)),
    ]
    for copy in kap_sends:
        copy.start()

    def x_copy(level, side):
        src, dst = (nx, 0) if side == 0 else (1, nx + 1)
        return remote(
            vv[level].at[src, :, pl.ds(8, ny)], vv[level].at[dst, :, pl.ds(8, ny)], xs_sem.at[level, side], xr_sem.at[level, side],
            toward("gx", 1 - 2 * side),
        )

    def y_copy(level, side, c):
        part = pl.ds(pl.multiple_of(c * CH, CH), CH)
        return remote(
            ys.at[level, 1 - side, :, part, :], yr.at[level, side, :, part, :],
            ys_sem.at[level, side, c], yr_sem.at[level, side, c], toward("gy", 1 - 2 * side),
        )

    def z_copy(level, side, c):
        return remote(
            zs.at[level, c], zr.at[level, side, c],
            zs_sem.at[level, side, c], zr_sem.at[level, side, c], toward("gz", 1 - 2 * side),
        )

    def emit(level, x, fields):
        for f in range(0, NF, 2):
            for t in range(TILES):
                full = jnp.concatenate([fields[f][t], fields[f + 1][t]], 0)
                high = full.astype(BF16)
                low = (full - high.astype(F32)).astype(BF16)
                hl[level][x, 0, f * 8:f * 8 + 16, t * 128:(t + 1) * 128] = high
                hl[level][x, 1, f * 8:f * 8 + 16, t * 128:(t + 1) * 128] = low
        if level < DEPTH:
            for f in range(NF):
                ys[level, 0, f, pl.ds(x, 1), :] = fields[f][0][0:1]
                ys[level, 1, f, pl.ds(x, 1), :] = fields[f][TILES - 1][7:8]

    def halves(level, x, count, t):
        part = slice(t * 128, (t + 1) * 128)
        return jnp.concatenate(
            [hl[level][pl.ds(x, count), h, :, part].reshape(count * BAND, 128) for h in range(2)], 1
        )

    def pack_chunk(level, c):
        result = [zero] * (NF // 2)
        for t in range(TILES):
            outer = jnp.dot(
                halves(level, c * CH, CH, t), gather[...], preferred_element_type=F32
            )
            for i in range(CH):
                for f in range(NF):
                    at_row = (i * NF + f) * 8
                    mask = (lane >> 1) == ((f % 2) * TILES + t) * CH + i
                    result[f // 2] = jnp.where(mask, outer[at_row:at_row + 8], result[f // 2])
        for m in range(NF // 2):
            zs[level, c, m] = result[m]

    def send_chunk(level, q, c):
        for side in range(2):
            y_copy(level, side, c).start()
        if level > 0:
            @pl.when(q == 0)
            def _():
                x_copy(level, 1).start()

            @pl.when(q == 1)
            def _():
                x_copy(level, 0).start()

        pack_chunk(level, c)
        for side in range(2):
            z_copy(level, side, c).start()

    def tiles_of(level, plane, f, by=0):
        return [vv[level][plane, f, pl.ds(8 + by + t * 8, 8), :] for t in range(TILES)]

    def order(q):
        return lax.rem(q * (chunks - 1), chunks)

    for copy in field_copies:
        copy.wait()
    for side in range(2):
        x_copy(0, side).start()

    def first_chunk(q, nothing):
        c = order(q)

        def plane(i, nothing):
            x = c * CH + i
            emit(0, x, [tiles_of(0, x + 1, f) for f in range(NF)])
            return nothing

        lax.fori_loop(0, CH, plane, 0, unroll=2)
        send_chunk(0, q, c)
        return nothing

    lax.fori_loop(0, chunks, first_chunk, 0)

    for copy in kap_sends:
        copy.wait_recv()

    def inside(axis, by):
        edge = 0 if by < 0 else size[axis] - 1
        return jnp.where(at[axis] == edge, 0.0, 1.0).astype(F32)

    def weights(x, nothing):
        own = [kp[x + 1, t * 8:(t + 1) * 8, :] for t in range(TILES)]
        x_low = jnp.where(x == 0, inside("gx", -1), 1.0)
        x_high = jnp.where(x == nx - 1, inside("gx", 1), 1.0)
        before = jnp.broadcast_to(kyr[0, pl.ds(x, 1), :] * inside("gy", -1), (8, 128))
        after = jnp.broadcast_to(kyr[1, pl.ds(x, 1), :] * inside("gy", 1), (8, 128))
        upper, lower = shifted_rows(own, before, after, row)
        turned = []
        for m in range(2):
            both = jnp.where(even, kzr[0, m] * inside("gz", -1), kzr[1, m] * inside("gz", 1))
            turned.append(pltpu.roll(both, lax.rem(128 - 2 * x, 128), 1))
        for t in range(TILES):
            pair = lane_roll(turned[t // 2], 127 - 64 * (t % 2))
            left, right = shifted_lanes(own[t], pair, lane)
            part = slice(t * 8, (t + 1) * 8)
            others = [
                kp[x + 2, part, :] * x_high, kp[x, part, :] * x_low,
                lower[t], upper[t], right, left,
            ]
            faces = [2.0 * own[t] * other * reciprocal(own[t] + other) for other in others]
            diagonal = faces[0]
            for face in faces[1:]:
                diagonal = diagonal + face
            scale = 2.5 * reciprocal(diagonal)
            for n in range(6):
                aa[x, n, part, :] = faces[n] * scale
        return nothing

    lax.fori_loop(0, nx, weights, 0, unroll=2)

    wide_lane = iota((16, 128), 1)
    second = jnp.where(iota((16, 128), 0) < 8, 0, TILES)
    groups = [((wide_lane >> 4) == second + t).astype(F32) for t in range(TILES)]

    for level in range(DEPTH):
        def chunk(q, nothing, level=level):
            c = order(q)
            for side in range(2):
                y_copy(level, side, c).wait_recv()
                z_copy(level, side, c).wait_recv()

            @pl.when(q == 0)
            def _():
                x_copy(level, 0).wait_recv()

            @pl.when(q == 1)
            def _():
                x_copy(level, 1).wait_recv()

            def outer_rows(i, nothing):
                x = c * CH + i
                for f in range(NF):
                    vv[level][x + 1, f, 7:8, :] = yr[level, 0, f, pl.ds(x, 1), :]
                    vv[level][x + 1, f, ny + 8:ny + 9, :] = yr[level, 1, f, pl.ds(x, 1), :]
                return nothing

            lax.fori_loop(0, CH, outer_rows, 0, unroll=4)
            columns = [[], []]
            for m in range(NF // 2):
                both = jnp.where(even, zr[level, 0, c, m], zr[level, 1, c, m])
                high = both.astype(BF16)
                low = (both - high.astype(F32)).astype(BF16)
                columns[0].append(jnp.concatenate([high, high], 0))
                columns[1].append(jnp.concatenate([low, low], 0))

            def unit(u, nothing):
                x0 = c * CH + u * UNIT
                masks = []
                for i in range(UNIT):
                    mine = ((wide_lane >> 1) & (CH - 1)) == u * UNIT + i
                    masks.append([jnp.where(mine, g, 0.0).astype(BF16) for g in groups])
                left_part = []
                for t in range(TILES):
                    outer = [
                        jnp.concatenate(
                            [columns[h][m] * masks[i][t] for i in range(UNIT) for m in range(NF // 2)], 0
                        )
                        for h in range(2)
                    ]
                    left_part.append(jnp.concatenate([halves(level, x0, UNIT, t)] + outer, 1))
                moved = jnp.dot(
                    jnp.concatenate(left_part, 0), shift[...], preferred_element_type=F32
                )
                for i in range(UNIT):
                    x = x0 + i
                    fields = []
                    for f in range(NF):
                        low = tiles_of(level, x, f)
                        high = tiles_of(level, x + 2, f)
                        upper = tiles_of(level, x + 1, f, -1)
                        lower = tiles_of(level, x + 1, f, 1)
                        tiles = []
                        for t in range(TILES):
                            at_row = ((t * UNIT + i) * NF + f) * 8
                            part = slice(t * 8, (t + 1) * 8)
                            total = aa[x, 0, part, :] * high[t]
                            total = total + aa[x, 1, part, :] * low[t]
                            total = total + aa[x, 2, part, :] * lower[t]
                            total = total + aa[x, 3, part, :] * upper[t]
                            total = total + aa[x, 4, part, :] * moved[at_row:at_row + 8, 128:]
                            total = total + aa[x, 5, part, :] * moved[at_row:at_row + 8, :128]
                            tiles.append(total)
                            if level + 1 < DEPTH:
                                vv[level + 1][x + 1, f, 8 + t * 8:16 + t * 8, :] = total
                        fields.append(tiles)
                    emit(level + 1, x, fields)
                return nothing

            lax.fori_loop(0, CH // UNIT, unit, 0)
            if level + 1 < DEPTH:
                send_chunk(level + 1, q, c)
            return nothing

        lax.fori_loop(0, chunks, chunk, 0)

    acc[...] = jnp.zeros_like(acc)

    def products(g, nothing):
        high, low = [
            jnp.concatenate(
                [
                    jnp.concatenate([ref[g * GROUP + i, h] for ref in hl], 0)
                    for i in range(GROUP)
                ],
                1,
            )
            for h in range(2)
        ]
        acc[...] += nt(jnp.concatenate([high, low], 0), high)
        return nothing

    lax.fori_loop(0, nx // GROUP, products, 0)

    same = (iota((ROWS, ROWS), 0) & 7) == (iota((ROWS, ROWS), 1) & 7)
    mixed = jnp.where(same, acc[0:ROWS] + 2.0 * acc[ROWS:], 0.0)
    pick_rows = ((iota((NC, ROWS), 1) >> 3) == iota((NC, ROWS), 0)).astype(F32)
    spread = ((iota((ROWS, 128), 0) >> 3) == iota((ROWS, 128), 1)).astype(F32)
    small = jnp.dot(pick_rows, mixed, precision=HIGH, preferred_element_type=F32)
    small = jnp.dot(small, spread, precision=HIGH, preferred_element_type=F32)
    message = small[0:8] + lane_roll(small[8:16], 32) + lane_roll(small[16:24], 64)

    sum_sends = []
    for number, count in enumerate((gx * gy, gz)):
        rank = ix * gy + iy if number == 0 else iz
        send, receive, slots = s_sem.at[number], r_sem.at[number], slot.at[number]

        def member(d):
            other = lax.rem(rank + d, count)
            if number:
                return other, {"gz": other}
            return other, {"gx": other // gy, "gy": lax.rem(other, gy)}

        msg[number] = message
        slots[rank] = message
        for d in range(1, count):
            copy = remote(
                msg.at[number], slots.at[rank], send.at[d], receive.at[rank], member(d)[1]
            )
            copy.start()
            sum_sends.append(copy)
        for d in range(1, count):
            source, device = member(d)
            remote(msg.at[number], slots.at[source], send.at[d], receive.at[source], device).wait_recv()
        message = slots[0]
        for d in range(1, count):
            message = message + slots[d]

    message = message * (0.5 / cells)
    lanes = iota((NC, 128), 1)
    rows = iota((NC, 128), 0)
    parts = [message, lane_roll(message, 96), lane_roll(message, 64)]
    half = jnp.where(lanes < NC, jnp.concatenate(parts, 0), 0.0)
    identity = (lanes == rows).astype(F32)
    padded = jnp.concatenate([half, jnp.zeros((128 - NC, 128), F32)], 0)
    matrix = half + nt(identity, padded, HIGH) + (lanes == rows + 32).astype(F32)
    pivots = jnp.ones((NC, 128), F32)

    def across(value, k):
        return jnp.broadcast_to(value[k:k + 1, :], (NC, 128))

    for first in range(0, NC, NF):
        columns = [
            jnp.broadcast_to(matrix[:, k:k + 1], (NC, 128)) for k in range(first, first + NF)
        ]
        for j in range(NF):
            k = first + j
            pivot = across(columns[j], k)
            pivots = jnp.where(rows == k, pivot, pivots)
            factors = jnp.where(rows > k, columns[j] * reciprocal(pivot), 0.0)
            for later in range(j + 1, NF):
                columns[later] = columns[later] - factors * across(columns[j], first + later)
            matrix = matrix - factors * across(matrix, k)
    matrix = matrix * (1.0 / jnp.sqrt(pivots))
    factor[...] = jnp.where((lanes >= rows) & (lanes < NC), matrix, 0.0)
    inverse = jnp.where(lanes <= rows, lane_roll(matrix, 96), 0.0)

    padded = jnp.concatenate([inverse, jnp.zeros((128 - NC, 128), F32)], 0)
    high = padded.astype(BF16)
    low = (padded - high.astype(F32)).astype(BF16)
    spread = spread.astype(BF16)
    for which, piece in enumerate((high, low)):
        wide = jnp.dot(spread, piece, preferred_element_type=F32).astype(BF16)
        wide = jnp.where(same, nt(wide, spread), 0.0).astype(BF16)
        wmat[which] = wide

    for copy in kap_sends + sum_sends:
        copy.wait_send()
    for level in range(DEPTH):
        for side in range(2):
            x_copy(level, side).wait_send()

            def drain(c, nothing, level=level, side=side):
                y_copy(level, side, c).wait_send()
                z_copy(level, side, c).wait_send()
                return nothing

            lax.fori_loop(0, chunks, drain, 0)


def solve_kernel(wmat, factor, hl0, hl1, hl2, hl3, q, r, held, sems):
    nx = hl0.shape[0]
    r[...] = factor[:, 0:NC]

    steps = nx // SPAN

    def out_copy(g):
        slot = lax.rem(g, SLOTS)
        return pltpu.make_async_copy(held.at[slot], q.at[:, pl.ds(g * SPAN, SPAN)], sems.at[slot])

    def planes(g, nothing):
        @pl.when(g >= SLOTS)
        def _():
            out_copy(g - SLOTS).wait()

        slot = lax.rem(g, SLOTS)
        high, low = [
            jnp.concatenate(
                [
                    jnp.concatenate([ref[g * SPAN + i, h] for ref in (hl0, hl1, hl2, hl3)], 0)
                    for i in range(SPAN)
                ],
                1,
            )
            for h in range(2)
        ]
        result = jnp.dot(wmat[0], high, preferred_element_type=F32)
        result = result + jnp.dot(wmat[0], low, preferred_element_type=F32)
        result = result + jnp.dot(wmat[1], high, preferred_element_type=F32)
        for f in range(NC):
            for i in range(SPAN):
                for t in range(TILES):
                    col = (i * TILES + t) * 128
                    held[slot, f, i, t * 8:(t + 1) * 8, :] = result[f * 8:(f + 1) * 8, col:col + 128]
        out_copy(g).start()
        return nothing

    lax.fori_loop(0, steps, planes, 0)

    def drain(g, nothing):
        out_copy(g).wait()
        return nothing

    lax.fori_loop(max(steps - SLOTS, 0), steps, drain, 0)


def on_device(sizes, right_sides, permeability):
    nx, ny, nz = permeability.shape
    chunks = nx // CH
    cells = float(nx * ny * nz * sizes[0] * sizes[1] * sizes[2])
    most = max(sizes[0] * sizes[1], sizes[2])
    dma = pltpu.SemaphoreType.DMA
    vmem = pl.BlockSpec(memory_space=pltpu.VMEM)
    *hl, wmat, factor = pl.pallas_call(
        functools.partial(basis_kernel, sizes, cells),
        out_shape=(
            *[pltpu.VMEM((nx, 2, BAND, TILES * 128), BF16)] * LEVELS,
            pltpu.VMEM((2, ROWS, ROWS), BF16),
            pltpu.VMEM((NC, 128), F32),
        ),
        in_specs=[pl.BlockSpec(memory_space=pl.ANY)] * 2,
        out_specs=(vmem,) * (LEVELS + 2),
        scratch_shapes=[
            pltpu.VMEM((nx + 2, ny, 128), F32),
            pltpu.VMEM((2, nx, 128), F32),
            pltpu.VMEM((2, nx, 128), F32),
            pltpu.VMEM((2, 8, 128), F32),
            pltpu.VMEM((2, 2, 8, 128), F32),
            *[pltpu.VMEM((nx + 2, NF, ny + 16, 128), F32)] * DEPTH,
            pltpu.VMEM((nx, 6, ny, 128), F32),
            pltpu.VMEM((DEPTH, 2, NF, nx, 128), F32),
            pltpu.VMEM((DEPTH, 2, NF, nx, 128), F32),
            pltpu.VMEM((DEPTH, chunks, NF // 2, 8, 128), F32),
            pltpu.VMEM((DEPTH, 2, chunks, NF // 2, 8, 128), F32),
            pltpu.VMEM((512, 256), BF16),
            pltpu.VMEM((256, 128), BF16),
            pltpu.VMEM((2 * ROWS, ROWS), F32),
            pltpu.VMEM((2, 8, 128), F32),
            pltpu.VMEM((2, most, 8, 128), F32),
            dma((NF + 1,)),
            dma((6,)), dma((6,)),
            dma((DEPTH, 2)), dma((DEPTH, 2)),
            dma((DEPTH, 2, chunks)), dma((DEPTH, 2, chunks)),
            dma((DEPTH, 2, chunks)), dma((DEPTH, 2, chunks)),
            dma((2, most)), dma((2, most)),
        ],
        compiler_params=pltpu.CompilerParams(
            collective_id=0, has_side_effects=True, vmem_limit_bytes=44 * 1024 * 1024
        ),
        name="basis",
    )(right_sides, permeability)
    return pl.pallas_call(
        solve_kernel,
        out_shape=(
            jax.ShapeDtypeStruct((NC, nx, ny, 128), F32),
            jax.ShapeDtypeStruct((NC, NC), F32),
        ),
        in_specs=[vmem] * (LEVELS + 2),
        out_specs=(pl.BlockSpec(memory_space=pl.ANY), vmem),
        scratch_shapes=[
            pltpu.VMEM((SLOTS, NC, SPAN, ny, 128), F32),
            dma((SLOTS,)),
        ],
        compiler_params=pltpu.CompilerParams(vmem_limit_bytes=12 * 1024 * 1024),
        name="solve",
    )(wmat, factor, *hl)


def solution(mesh):
    sizes = tuple(mesh.shape[axis] for axis in ("gx", "gy", "gz"))
    return jax.shard_map(
        functools.partial(on_device, sizes),
        mesh=mesh,
        in_specs=(P(None, "gx", "gy", "gz"), P("gx", "gy", "gz")),
        out_specs=(P(None, "gx", "gy", "gz"), P()),
        check_vma=False,
    )
```

```python
import functools

import jax
import jax.numpy as jnp
from jax import lax
from jax.experimental import pallas as pl
from jax.experimental.pallas import tpu as pltpu
from jax.sharding import PartitionSpec as P

NF = 6
DEPTH = 3
LEVELS = DEPTH + 1
NC = NF * LEVELS
CH = 8
TILES = 4
ROWS = NC * 8
BAND = NF * 8
UNIT = 4
GROUP = 8
SPAN = 4
SLOTS = 4
MESH = pl.DeviceIdType.MESH
F32 = jnp.float32
BF16 = jnp.bfloat16
HIGH = lax.Precision.HIGHEST


def iota(shape, dim):
    return lax.broadcasted_iota(jnp.int32, shape, dim)


def nt(left, right, precision=None):
    return lax.dot_general(
        left, right, (((1,), (1,)), ((), ())), precision=precision, preferred_element_type=F32
    )


def reciprocal(value):
    guess = pl.reciprocal(value, approx=True)
    return guess * (2.0 - value * guess)


def lane_roll(value, amount):
    return pltpu.roll(value, amount % 128, 1)


def shifted_rows(tiles, before, after, row):
    rolled = [pltpu.roll(v, 1, 0) for v in tiles]
    upper = [jnp.where(row == 0, p, r) for p, r in zip([before] + rolled[:-1], rolled)]
    rolled = [pltpu.roll(v, 7, 0) for v in tiles]
    lower = [jnp.where(row == 7, n, r) for n, r in zip(rolled[1:] + [after], rolled)]
    return upper, lower


def shifted_lanes(value, pair, lane):
    left = lane_roll(jnp.where(lane == 127, pair, value), 1)
    right = lane_roll(jnp.where(lane == 0, pair, value), 127)
    return left, right


def basis_kernel(
    sizes, cells, rs, kap, hl0, hl1, hl2, hl3, wmat, factor,
    kp, kys, kyr, kzs, kzr, v0, v1, v2, aa, ys, yr, zs, zr, shift, gather, acc, msg, slot,
    load_sem, ks_sem, kr_sem, xs_sem, xr_sem, ys_sem, yr_sem, zs_sem, zr_sem,
    s_sem, r_sem,
):
    hl = (hl0, hl1, hl2, hl3)
    vv = (v0, v1, v2)
    gx, gy, gz = sizes
    nx, ny = kp.shape[0] - 2, kp.shape[1]
    chunks = nx // CH
    ix, iy, iz = lax.axis_index("gx"), lax.axis_index("gy"), lax.axis_index("gz")
    at = {"gx": ix, "gy": iy, "gz": iz}
    size = {"gx": gx, "gy": gy, "gz": gz}

    def toward(axis, by):
        return {axis: lax.rem(at[axis] + (by + size[axis]), size[axis])}

    kap_copy = pltpu.make_async_copy(kap, kp.at[pl.ds(1, nx)], load_sem.at[NF])
    kap_copy.start()
    field_copies = []
    for f in range(NF):
        copy = pltpu.make_async_copy(rs.at[f], v0.at[pl.ds(1, nx), f, pl.ds(8, ny)], load_sem.at[f])
        copy.start()
        field_copies.append(copy)

    n1 = gx * gy
    rank1 = ix * gy + iy
    barrier = pltpu.get_barrier_semaphore()
    greeted = []
    for d in range(1, n1):
        other = lax.rem(rank1 + d, n1)
        greeted.append({"gx": other // gy, "gy": lax.rem(other, gy)})
    greeted += [{"gz": lax.rem(iz + d, gz)} for d in range(1, gz)]
    for device in greeted:
        pl.semaphore_signal(barrier, inc=1, device_id=device, device_id_type=MESH)

    lane = iota((8, 128), 1)
    row = iota((8, 128), 0)
    even = (lane & 1) == 0
    zero = jnp.zeros((8, 128), F32)

    def remote(src, dst, send, recv, device):
        return pltpu.make_async_remote_copy(
            src_ref=src, dst_ref=dst, send_sem=send, recv_sem=recv,
            device_id=device, device_id_type=MESH,
        )

    source, target = iota((256, 256), 0) & 127, iota((256, 256), 1)
    wanted = jnp.where(target < 128, target - 1, target - 127)
    shift[0:256] = (source == wanted).astype(F32).astype(BF16)
    wanted = jnp.where((source & 1) == 0, 0, 255)
    shift[256:512] = (target == wanted).astype(F32).astype(BF16)
    source, target = iota((256, 128), 0) & 127, iota((256, 128), 1)
    wanted = jnp.where((target & 1) == 0, 127, 0)
    gather[...] = (source == wanted).astype(F32).astype(BF16)

    kap_copy.wait()

    def pack_kap(x, carry):
        tiles = [kp[x + 1, t * 8:(t + 1) * 8, :] for t in range(TILES)]
        kys[0, pl.ds(x, 1), :] = tiles[0][0:1]
        kys[1, pl.ds(x, 1), :] = tiles[3][7:8]
        result = []
        for m in range(2):
            both = jnp.where(lane < 64, lane_roll(tiles[2 * m], 1), lane_roll(tiles[2 * m + 1], 65))
            both = pltpu.roll(both, 2 * x, 1)
            result.append(jnp.where(((lane >> 1) & 31) == x, both, carry[m]))
        return tuple(result)

    packed = lax.fori_loop(0, nx, pack_kap, (zero, zero), unroll=8)
    for m in range(2):
        kzs[m] = packed[m]
    pl.semaphore_wait(barrier, n1 + gz - 2)

    kap_sends = [
        remote(kp.at[nx], kp.at[0], ks_sem.at[0], kr_sem.at[0], toward("gx", 1)),
        remote(kp.at[1], kp.at[nx + 1], ks_sem.at[1], kr_sem.at[1], toward("gx", -1)),
        remote(kys.at[1], kyr.at[0], ks_sem.at[2], kr_sem.at[2], toward("gy", 1)),
        remote(kys.at[0], kyr.at[1], ks_sem.at[3], kr_sem.at[3], toward("gy", -1)),
        remote(kzs, kzr.at[0], ks_sem.at[4], kr_sem.at[4], toward("gz", 1)),
        remote(kzs, kzr.at[1], ks_sem.at[5], kr_sem.at[5], toward("gz", -1)),
    ]
    for copy in kap_sends:
        copy.start()

    def x_copy(level, side):
        src, dst = (nx, 0) if side == 0 else (1, nx + 1)
        return remote(
            vv[level].at[src, :, pl.ds(8, ny)], vv[level].at[dst, :, pl.ds(8, ny)], xs_sem.at[level, side], xr_sem.at[level, side],
            toward("gx", 1 - 2 * side),
        )

    def y_copy(level, side, c):
        part = pl.ds(pl.multiple_of(c * CH, CH), CH)
        return remote(
            ys.at[level, 1 - side, :, part, :], yr.at[level, side, :, part, :],
            ys_sem.at[level, side, c], yr_sem.at[level, side, c], toward("gy", 1 - 2 * side),
        )

    def z_copy(level, side, c):
        return remote(
            zs.at[level, c], zr.at[level, side, c],
            zs_sem.at[level, side, c], zr_sem.at[level, side, c], toward("gz", 1 - 2 * side),
        )

    def emit(level, x, fields):
        for f in range(0, NF, 2):
            for t in range(TILES):
                full = jnp.concatenate([fields[f][t], fields[f + 1][t]], 0)
                high = full.astype(BF16)
                low = (full - high.astype(F32)).astype(BF16)
                hl[level][x, 0, f * 8:f * 8 + 16, t * 128:(t + 1) * 128] = high
                hl[level][x, 1, f * 8:f * 8 + 16, t * 128:(t + 1) * 128] = low
        if level < DEPTH:
            for f in range(NF):
                ys[level, 0, f, pl.ds(x, 1), :] = fields[f][0][0:1]
                ys[level, 1, f, pl.ds(x, 1), :] = fields[f][TILES - 1][7:8]

    def halves(level, x, count, t):
        part = slice(t * 128, (t + 1) * 128)
        return jnp.concatenate(
            [hl[level][pl.ds(x, count), h, :, part].reshape(count * BAND, 128) for h in range(2)], 1
        )

    def pack_chunk(level, c):
        result = [zero] * (NF // 2)
        for t in range(TILES):
            outer = jnp.dot(
                halves(level, c * CH, CH, t), gather[...], preferred_element_type=F32
            )
            for i in range(CH):
                for f in range(NF):
                    at_row = (i * NF + f) * 8
                    mask = (lane >> 1) == ((f % 2) * TILES + t) * CH + i
                    result[f // 2] = jnp.where(mask, outer[at_row:at_row + 8], result[f // 2])
        for m in range(NF // 2):
            zs[level, c, m] = result[m]

    def send_chunk(level, q, c):
        for side in range(2):
            y_copy(level, side, c).start()
        if level > 0:
            @pl.when(q == 0)
            def _():
                x_copy(level, 1).start()

            @pl.when(q == 1)
            def _():
                x_copy(level, 0).start()

        pack_chunk(level, c)
        for side in range(2):
            z_copy(level, side, c).start()

    def tiles_of(level, plane, f, by=0):
        return [vv[level][plane, f, pl.ds(8 + by + t * 8, 8), :] for t in range(TILES)]

    def order(q):
        return lax.rem(q * (chunks - 1), chunks)

    for copy in field_copies:
        copy.wait()
    for side in range(2):
        x_copy(0, side).start()

    def first_chunk(q, nothing):
        c = order(q)

        def plane(i, nothing):
            x = c * CH + i
            emit(0, x, [tiles_of(0, x + 1, f) for f in range(NF)])
            return nothing

        lax.fori_loop(0, CH, plane, 0, unroll=2)
        send_chunk(0, q, c)
        return nothing

    lax.fori_loop(0, chunks, first_chunk, 0)

    for copy in kap_sends:
        copy.wait_recv()

    def inside(axis, by):
        edge = 0 if by < 0 else size[axis] - 1
        return jnp.where(at[axis] == edge, 0.0, 1.0).astype(F32)

    def weights(x, nothing):
        own = [kp[x + 1, t * 8:(t + 1) * 8, :] for t in range(TILES)]
        x_low = jnp.where(x == 0, inside("gx", -1), 1.0)
        x_high = jnp.where(x == nx - 1, inside("gx", 1), 1.0)
        before = jnp.broadcast_to(kyr[0, pl.ds(x, 1), :] * inside("gy", -1), (8, 128))
        after = jnp.broadcast_to(kyr[1, pl.ds(x, 1), :] * inside("gy", 1), (8, 128))
        upper, lower = shifted_rows(own, before, after, row)
        turned = []
        for m in range(2):
            both = jnp.where(even, kzr[0, m] * inside("gz", -1), kzr[1, m] * inside("gz", 1))
            turned.append(pltpu.roll(both, lax.rem(128 - 2 * x, 128), 1))
        for t in range(TILES):
            pair = lane_roll(turned[t // 2], 127 - 64 * (t % 2))
            left, right = shifted_lanes(own[t], pair, lane)
            part = slice(t * 8, (t + 1) * 8)
            others = [
                kp[x + 2, part, :] * x_high, kp[x, part, :] * x_low,
                lower[t], upper[t], right, left,
            ]
            faces = [2.0 * own[t] * other * reciprocal(own[t] + other) for other in others]
            diagonal = faces[0]
            for face in faces[1:]:
                diagonal = diagonal + face
            scale = 2.5 * reciprocal(diagonal)
            for n in range(6):
                aa[x, n, part, :] = faces[n] * scale
        return nothing

    lax.fori_loop(0, nx, weights, 0, unroll=4)

    wide_lane = iota((16, 128), 1)
    second = jnp.where(iota((16, 128), 0) < 8, 0, TILES)
    groups = [((wide_lane >> 4) == second + t).astype(F32) for t in range(TILES)]

    for level in range(DEPTH):
        def chunk(q, nothing, level=level):
            c = order(q)
            for side in range(2):
                y_copy(level, side, c).wait_recv()
                z_copy(level, side, c).wait_recv()

            @pl.when(q == 0)
            def _():
                x_copy(level, 0).wait_recv()

            @pl.when(q == 1)
            def _():
                x_copy(level, 1).wait_recv()

            def outer_rows(i, nothing):
                x = c * CH + i
                for f in range(NF):
                    vv[level][x + 1, f, 7:8, :] = yr[level, 0, f, pl.ds(x, 1), :]
                    vv[level][x + 1, f, ny + 8:ny + 9, :] = yr[level, 1, f, pl.ds(x, 1), :]
                return nothing

            lax.fori_loop(0, CH, outer_rows, 0, unroll=4)
            columns = [[], []]
            for m in range(NF // 2):
                both = jnp.where(even, zr[level, 0, c, m], zr[level, 1, c, m])
                high = both.astype(BF16)
                low = (both - high.astype(F32)).astype(BF16)
                columns[0].append(jnp.concatenate([high, high], 0))
                columns[1].append(jnp.concatenate([low, low], 0))

            def unit(u, nothing):
                x0 = c * CH + u * UNIT
                masks = []
                for i in range(UNIT):
                    mine = ((wide_lane >> 1) & (CH - 1)) == u * UNIT + i
                    masks.append([jnp.where(mine, g, 0.0).astype(BF16) for g in groups])
                left_part = []
                for t in range(TILES):
                    outer = [
                        jnp.concatenate(
                            [columns[h][m] * masks[i][t] for i in range(UNIT) for m in range(NF // 2)], 0
                        )
                        for h in range(2)
                    ]
                    left_part.append(jnp.concatenate([halves(level, x0, UNIT, t)] + outer, 1))
                moved = jnp.dot(
                    jnp.concatenate(left_part, 0), shift[...], preferred_element_type=F32
                )
                for i in range(UNIT):
                    x = x0 + i
                    fields = []
                    for f in range(NF):
                        low = tiles_of(level, x, f)
                        high = tiles_of(level, x + 2, f)
                        upper = tiles_of(level, x + 1, f, -1)
                        lower = tiles_of(level, x + 1, f, 1)
                        tiles = []
                        for t in range(TILES):
                            at_row = ((t * UNIT + i) * NF + f) * 8
                            part = slice(t * 8, (t + 1) * 8)
                            total = aa[x, 0, part, :] * high[t]
                            total = total + aa[x, 1, part, :] * low[t]
                            total = total + aa[x, 2, part, :] * lower[t]
                            total = total + aa[x, 3, part, :] * upper[t]
                            total = total + aa[x, 4, part, :] * moved[at_row:at_row + 8, 128:]
                            total = total + aa[x, 5, part, :] * moved[at_row:at_row + 8, :128]
                            tiles.append(total)
                            if level + 1 < DEPTH:
                                vv[level + 1][x + 1, f, 8 + t * 8:16 + t * 8, :] = total
                        fields.append(tiles)
                    emit(level + 1, x, fields)
                return nothing

            lax.fori_loop(0, CH // UNIT, unit, 0)
            if level + 1 < DEPTH:
                send_chunk(level + 1, q, c)
            return nothing

        lax.fori_loop(0, chunks, chunk, 0)

    acc[...] = jnp.zeros_like(acc)

    def products(g, nothing):
        high, low = [
            jnp.concatenate(
                [
                    jnp.concatenate([ref[g * GROUP + i, h] for ref in hl], 0)
                    for i in range(GROUP)
                ],
                1,
            )
            for h in range(2)
        ]
        acc[...] += nt(jnp.concatenate([high, low], 0), high)
        return nothing

    lax.fori_loop(0, nx // GROUP, products, 0)

    same = (iota((ROWS, ROWS), 0) & 7) == (iota((ROWS, ROWS), 1) & 7)
    mixed = jnp.where(same, acc[0:ROWS] + 2.0 * acc[ROWS:], 0.0)
    pick_rows = ((iota((NC, ROWS), 1) >> 3) == iota((NC, ROWS), 0)).astype(F32)
    spread = ((iota((ROWS, 128), 0) >> 3) == iota((ROWS, 128), 1)).astype(F32)
    small = jnp.dot(pick_rows, mixed, precision=HIGH, preferred_element_type=F32)
    small = jnp.dot(small, spread, precision=HIGH, preferred_element_type=F32)
    message = small[0:8] + lane_roll(small[8:16], 32) + lane_roll(small[16:24], 64)

    sum_sends = []
    for number, count in enumerate((gx * gy, gz)):
        rank = ix * gy + iy if number == 0 else iz
        send, receive, slots = s_sem.at[number], r_sem.at[number], slot.at[number]

        def member(d):
            other = lax.rem(rank + d, count)
            if number:
                return other, {"gz": other}
            return other, {"gx": other // gy, "gy": lax.rem(other, gy)}

        msg[number] = message
        slots[rank] = message
        for d in range(1, count):
            copy = remote(
                msg.at[number], slots.at[rank], send.at[d], receive.at[rank], member(d)[1]
            )
            copy.start()
            sum_sends.append(copy)
        for d in range(1, count):
            source, device = member(d)
            remote(msg.at[number], slots.at[source], send.at[d], receive.at[source], device).wait_recv()
        message = slots[0]
        for d in range(1, count):
            message = message + slots[d]

    message = message * (0.5 / cells)
    lanes = iota((NC, 128), 1)
    rows = iota((NC, 128), 0)
    parts = [message, lane_roll(message, 96), lane_roll(message, 64)]
    half = jnp.where(lanes < NC, jnp.concatenate(parts, 0), 0.0)
    identity = (lanes == rows).astype(F32)
    padded = jnp.concatenate([half, jnp.zeros((128 - NC, 128), F32)], 0)
    matrix = half + nt(identity, padded, HIGH) + (lanes == rows + 32).astype(F32)
    pivots = jnp.ones((NC, 128), F32)

    def across(value, k):
        return jnp.broadcast_to(value[k:k + 1, :], (NC, 128))

    for first in range(0, NC, NF):
        columns = [
            jnp.broadcast_to(matrix[:, k:k + 1], (NC, 128)) for k in range(first, first + NF)
        ]
        for j in range(NF):
            k = first + j
            pivot = across(columns[j], k)
            pivots = jnp.where(rows == k, pivot, pivots)
            factors = jnp.where(rows > k, columns[j] * reciprocal(pivot), 0.0)
            for later in range(j + 1, NF):
                columns[later] = columns[later] - factors * across(columns[j], first + later)
            matrix = matrix - factors * across(matrix, k)
    matrix = matrix * (1.0 / jnp.sqrt(pivots))
    factor[...] = jnp.where((lanes >= rows) & (lanes < NC), matrix, 0.0)
    inverse = jnp.where(lanes <= rows, lane_roll(matrix, 96), 0.0)

    padded = jnp.concatenate([inverse, jnp.zeros((128 - NC, 128), F32)], 0)
    high = padded.astype(BF16).astype(F32)
    both = (high + lane_roll((padded - high).astype(BF16).astype(F32), NC)).astype(BF16)
    tall = jnp.dot(spread.astype(BF16), both, preferred_element_type=F32).astype(BF16)
    place, chosen = iota((3 * ROWS, 128), 0), iota((3 * ROWS, 128), 1)
    kind = (place >= 3 * BAND).astype(jnp.int32)
    for level in range(2, LEVELS):
        kind = kind + (place >= 3 * BAND * level).astype(jnp.int32)
    inner = place - 3 * BAND * kind
    place = kind * BAND + jnp.where(
        inner < BAND, inner, jnp.where(inner < 2 * BAND, inner - BAND, inner - 2 * BAND + ROWS)
    )
    wide = nt(tall, ((place >> 3) == chosen).astype(F32).astype(BF16))
    same = (iota((ROWS, 3 * ROWS), 0) & 7) == (iota((ROWS, 3 * ROWS), 1) & 7)
    wmat[...] = jnp.where(same, wide, 0.0).astype(BF16)

    for copy in kap_sends + sum_sends:
        copy.wait_send()
    for level in range(DEPTH):
        for side in range(2):
            x_copy(level, side).wait_send()

            def drain(c, nothing, level=level, side=side):
                y_copy(level, side, c).wait_send()
                z_copy(level, side, c).wait_send()
                return nothing

            lax.fori_loop(0, chunks, drain, 0)


def solve_kernel(wmat, factor, hl0, hl1, hl2, hl3, q, r, held, sems):
    nx = hl0.shape[0]
    r[...] = factor[:, 0:NC]

    steps = nx // SPAN

    def out_copy(g):
        slot = lax.rem(g, SLOTS)
        return pltpu.make_async_copy(held.at[slot], q.at[:, pl.ds(g * SPAN, SPAN)], sems.at[slot])

    def planes(g, nothing):
        @pl.when(g >= SLOTS)
        def _():
            out_copy(g - SLOTS).wait()

        slot = lax.rem(g, SLOTS)
        data = []
        for ref in (hl0, hl1, hl2, hl3):
            high, low = [
                jnp.concatenate([ref[g * SPAN + i, h] for i in range(SPAN)], 1) for h in range(2)
            ]
            data += [high, low, high]
        data = jnp.concatenate(data, 0)
        result = None
        for start in range(0, 3 * ROWS, 256):
            stop = min(start + 256, 3 * ROWS)
            above = start // (3 * BAND) * BAND
            part = jnp.dot(
                wmat[above:, start:stop], data[start:stop], preferred_element_type=F32
            )
            if result is not None:
                part = jnp.concatenate([result[:above], result[above:] + part], 0)
            result = part
        for f in range(NC):
            for i in range(SPAN):
                for t in range(TILES):
                    col = (i * TILES + t) * 128
                    held[slot, f, i, t * 8:(t + 1) * 8, :] = result[f * 8:(f + 1) * 8, col:col + 128]
        out_copy(g).start()
        return nothing

    lax.fori_loop(0, steps, planes, 0)

    def drain(g, nothing):
        out_copy(g).wait()
        return nothing

    lax.fori_loop(max(steps - SLOTS, 0), steps, drain, 0)


def on_device(sizes, right_sides, permeability):
    nx, ny, nz = permeability.shape
    chunks = nx // CH
    cells = float(nx * ny * nz * sizes[0] * sizes[1] * sizes[2])
    most = max(sizes[0] * sizes[1], sizes[2])
    dma = pltpu.SemaphoreType.DMA
    vmem = pl.BlockSpec(memory_space=pltpu.VMEM)
    *hl, wmat, factor = pl.pallas_call(
        functools.partial(basis_kernel, sizes, cells),
        out_shape=(
            *[pltpu.VMEM((nx, 2, BAND, TILES * 128), BF16)] * LEVELS,
            pltpu.VMEM((ROWS, 3 * ROWS), BF16),
            pltpu.VMEM((NC, 128), F32),
        ),
        in_specs=[pl.BlockSpec(memory_space=pl.ANY)] * 2,
        out_specs=(vmem,) * (LEVELS + 2),
        scratch_shapes=[
            pltpu.VMEM((nx + 2, ny, 128), F32),
            pltpu.VMEM((2, nx, 128), F32),
            pltpu.VMEM((2, nx, 128), F32),
            pltpu.VMEM((2, 8, 128), F32),
            pltpu.VMEM((2, 2, 8, 128), F32),
            *[pltpu.VMEM((nx + 2, NF, ny + 16, 128), F32)] * DEPTH,
            pltpu.VMEM((nx, 6, ny, 128), F32),
            pltpu.VMEM((DEPTH, 2, NF, nx, 128), F32),
            pltpu.VMEM((DEPTH, 2, NF, nx, 128), F32),
            pltpu.VMEM((DEPTH, chunks, NF // 2, 8, 128), F32),
            pltpu.VMEM((DEPTH, 2, chunks, NF // 2, 8, 128), F32),
            pltpu.VMEM((512, 256), BF16),
            pltpu.VMEM((256, 128), BF16),
            pltpu.VMEM((2 * ROWS, ROWS), F32),
            pltpu.VMEM((2, 8, 128), F32),
            pltpu.VMEM((2, most, 8, 128), F32),
            dma((NF + 1,)),
            dma((6,)), dma((6,)),
            dma((DEPTH, 2)), dma((DEPTH, 2)),
            dma((DEPTH, 2, chunks)), dma((DEPTH, 2, chunks)),
            dma((DEPTH, 2, chunks)), dma((DEPTH, 2, chunks)),
            dma((2, most)), dma((2, most)),
        ],
        compiler_params=pltpu.CompilerParams(
            collective_id=0, has_side_effects=True, vmem_limit_bytes=44 * 1024 * 1024
        ),
        name="basis",
    )(right_sides, permeability)
    return pl.pallas_call(
        solve_kernel,
        out_shape=(
            jax.ShapeDtypeStruct((NC, nx, ny, 128), F32),
            jax.ShapeDtypeStruct((NC, NC), F32),
        ),
        in_specs=[vmem] * (LEVELS + 2),
        out_specs=(pl.BlockSpec(memory_space=pl.ANY), vmem),
        scratch_shapes=[
            pltpu.VMEM((SLOTS, NC, SPAN, ny, 128), F32),
            dma((SLOTS,)),
        ],
        compiler_params=pltpu.CompilerParams(vmem_limit_bytes=12 * 1024 * 1024),
        name="solve",
    )(wmat, factor, *hl)


def solution(mesh):
    sizes = tuple(mesh.shape[axis] for axis in ("gx", "gy", "gz"))
    return jax.shard_map(
        functools.partial(on_device, sizes),
        mesh=mesh,
        in_specs=(P(None, "gx", "gy", "gz"), P("gx", "gy", "gz")),
        out_specs=(P(None, "gx", "gy", "gz"), P()),
        check_vma=False,
    )
```

```python
import functools

import jax
import jax.numpy as jnp
from jax import lax
from jax.experimental import pallas as pl
from jax.experimental.pallas import tpu as pltpu
from jax.sharding import PartitionSpec as P

NF = 6
DEPTH = 3
LEVELS = DEPTH + 1
NC = NF * LEVELS
CH = 8
TILES = 4
ROWS = NC * 8
BAND = NF * 8
UNIT = 4
GROUP = 8
SPAN = 4
SLOTS = 4
MESH = pl.DeviceIdType.MESH
F32 = jnp.float32
BF16 = jnp.bfloat16
HIGH = lax.Precision.HIGHEST


def iota(shape, dim):
    return lax.broadcasted_iota(jnp.int32, shape, dim)


def nt(left, right, precision=None):
    return lax.dot_general(
        left, right, (((1,), (1,)), ((), ())), precision=precision, preferred_element_type=F32
    )


def reciprocal(value):
    guess = pl.reciprocal(value, approx=True)
    return guess * (2.0 - value * guess)


def lane_roll(value, amount):
    return pltpu.roll(value, amount % 128, 1)


def shifted_rows(tiles, before, after, row):
    rolled = [pltpu.roll(v, 1, 0) for v in tiles]
    upper = [jnp.where(row == 0, p, r) for p, r in zip([before] + rolled[:-1], rolled)]
    rolled = [pltpu.roll(v, 7, 0) for v in tiles]
    lower = [jnp.where(row == 7, n, r) for n, r in zip(rolled[1:] + [after], rolled)]
    return upper, lower


def shifted_lanes(value, pair, lane):
    left = lane_roll(jnp.where(lane == 127, pair, value), 1)
    right = lane_roll(jnp.where(lane == 0, pair, value), 127)
    return left, right


def basis_kernel(
    sizes, cells, rs, kap, hl0, hl1, hl2, hl3, wmat, factor,
    kp, kys, kyr, kzs, kzr, v0, v1, v2, aa, ys, yr, zs, zr, shift, gather, acc, msg, slot,
    load_sem, ks_sem, kr_sem, xs_sem, xr_sem, ys_sem, yr_sem, zs_sem, zr_sem,
    s_sem, r_sem,
):
    hl = (hl0, hl1, hl2, hl3)
    vv = (v0, v1, v2)
    gx, gy, gz = sizes
    nx, ny = kp.shape[0] - 2, kp.shape[1]
    chunks = nx // CH
    ix, iy, iz = lax.axis_index("gx"), lax.axis_index("gy"), lax.axis_index("gz")
    at = {"gx": ix, "gy": iy, "gz": iz}
    size = {"gx": gx, "gy": gy, "gz": gz}

    def toward(axis, by):
        return {axis: lax.rem(at[axis] + (by + size[axis]), size[axis])}

    kap_copy = pltpu.make_async_copy(kap, kp.at[pl.ds(1, nx)], load_sem.at[NF])
    kap_copy.start()
    field_copies = []
    for f in range(NF):
        copy = pltpu.make_async_copy(rs.at[f], v0.at[pl.ds(1, nx), f, pl.ds(8, ny)], load_sem.at[f])
        copy.start()
        field_copies.append(copy)

    n1 = gx * gy
    rank1 = ix * gy + iy
    barrier = pltpu.get_barrier_semaphore()
    greeted = []
    for d in range(1, n1):
        other = lax.rem(rank1 + d, n1)
        greeted.append({"gx": other // gy, "gy": lax.rem(other, gy)})
    greeted += [{"gz": lax.rem(iz + d, gz)} for d in range(1, gz)]
    for device in greeted:
        pl.semaphore_signal(barrier, inc=1, device_id=device, device_id_type=MESH)

    lane = iota((8, 128), 1)
    row = iota((8, 128), 0)
    even = (lane & 1) == 0
    zero = jnp.zeros((8, 128), F32)

    def remote(src, dst, send, recv, device):
        return pltpu.make_async_remote_copy(
            src_ref=src, dst_ref=dst, send_sem=send, recv_sem=recv,
            device_id=device, device_id_type=MESH,
        )

    source, target = iota((256, 256), 0) & 127, iota((256, 256), 1)
    wanted = jnp.where(target < 128, target - 1, target - 127)
    shift[0:256] = (source == wanted).astype(F32).astype(BF16)
    wanted = jnp.where((source & 1) == 0, 0, 255)
    shift[256:512] = (target == wanted).astype(F32).astype(BF16)
    source, target = iota((256, 128), 0) & 127, iota((256, 128), 1)
    wanted = jnp.where((target & 1) == 0, 127, 0)
    gather[...] = (source == wanted).astype(F32).astype(BF16)

    kap_copy.wait()

    def pack_kap(x, carry):
        tiles = [kp[x + 1, t * 8:(t + 1) * 8, :] for t in range(TILES)]
        kys[0, pl.ds(x, 1), :] = tiles[0][0:1]
        kys[1, pl.ds(x, 1), :] = tiles[3][7:8]
        result = []
        for m in range(2):
            both = jnp.where(lane < 64, lane_roll(tiles[2 * m], 1), lane_roll(tiles[2 * m + 1], 65))
            both = pltpu.roll(both, 2 * x, 1)
            result.append(jnp.where(((lane >> 1) & 31) == x, both, carry[m]))
        return tuple(result)

    packed = lax.fori_loop(0, nx, pack_kap, (zero, zero), unroll=8)
    for m in range(2):
        kzs[m] = packed[m]
    pl.semaphore_wait(barrier, n1 + gz - 2)

    kap_sends = [
        remote(kp.at[nx], kp.at[0], ks_sem.at[0], kr_sem.at[0], toward("gx", 1)),
        remote(kp.at[1], kp.at[nx + 1], ks_sem.at[1], kr_sem.at[1], toward("gx", -1)),
        remote(kys.at[1], kyr.at[0], ks_sem.at[2], kr_sem.at[2], toward("gy", 1)),
        remote(kys.at[0], kyr.at[1], ks_sem.at[3], kr_sem.at[3], toward("gy", -1)),
        remote(kzs, kzr.at[0], ks_sem.at[4], kr_sem.at[4], toward("gz", 1)),
        remote(kzs, kzr.at[1], ks_sem.at[5], kr_sem.at[5], toward("gz", -1)),
    ]
    for copy in kap_sends:
        copy.start()

    def x_copy(level, side):
        src, dst = (nx, 0) if side == 0 else (1, nx + 1)
        return remote(
            vv[level].at[src, :, pl.ds(8, ny)], vv[level].at[dst, :, pl.ds(8, ny)], xs_sem.at[level, side], xr_sem.at[level, side],
            toward("gx", 1 - 2 * side),
        )

    def y_copy(level, side, c):
        part = pl.ds(pl.multiple_of(c * CH, CH), CH)
        return remote(
            ys.at[level, 1 - side, :, part, :], yr.at[level, side, :, part, :],
            ys_sem.at[level, side, c], yr_sem.at[level, side, c], toward("gy", 1 - 2 * side),
        )

    def z_copy(level, side, c):
        return remote(
            zs.at[level, c], zr.at[level, side, c],
            zs_sem.at[level, side, c], zr_sem.at[level, side, c], toward("gz", 1 - 2 * side),
        )

    def emit(level, x, fields):
        for f in range(0, NF, 2):
            for t in range(TILES):
                full = jnp.concatenate([fields[f][t], fields[f + 1][t]], 0)
                high = full.astype(BF16)
                low = (full - high.astype(F32)).astype(BF16)
                hl[level][x, 0, f * 8:f * 8 + 16, t * 128:(t + 1) * 128] = high
                hl[level][x, 1, f * 8:f * 8 + 16, t * 128:(t + 1) * 128] = low
        if level < DEPTH:
            for f in range(NF):
                ys[level, 0, f, pl.ds(x, 1), :] = fields[f][0][0:1]
                ys[level, 1, f, pl.ds(x, 1), :] = fields[f][TILES - 1][7:8]

    def halves(level, x, count, t):
        part = slice(t * 128, (t + 1) * 128)
        return jnp.concatenate(
            [hl[level][pl.ds(x, count), h, :, part].reshape(count * BAND, 128) for h in range(2)], 1
        )

    def pack_chunk(level, c):
        result = [zero] * (NF // 2)
        for t in range(TILES):
            outer = jnp.dot(
                halves(level, c * CH, CH, t), gather[...], preferred_element_type=F32
            )
            for i in range(CH):
                for f in range(NF):
                    at_row = (i * NF + f) * 8
                    mask = (lane >> 1) == ((f % 2) * TILES + t) * CH + i
                    result[f // 2] = jnp.where(mask, outer[at_row:at_row + 8], result[f // 2])
        for m in range(NF // 2):
            zs[level, c, m] = result[m]

    def send_chunk(level, q, c):
        for side in range(2):
            y_copy(level, side, c).start()
        if level > 0:
            @pl.when(q == 0)
            def _():
                x_copy(level, 1).start()

        pack_chunk(level, c)
        for side in range(2):
            z_copy(level, side, c).start()

    def tiles_of(level, plane, f, by=0):
        return [vv[level][plane, f, pl.ds(8 + by + t * 8, 8), :] for t in range(TILES)]

    def order(q):
        return lax.rem(q * (chunks - 1), chunks)

    for copy in field_copies:
        copy.wait()
    for side in range(2):
        x_copy(0, side).start()

    def first_chunk(q, nothing):
        c = order(q)

        def plane(i, nothing):
            x = c * CH + i
            emit(0, x, [tiles_of(0, x + 1, f) for f in range(NF)])
            return nothing

        lax.fori_loop(0, CH, plane, 0, unroll=2)
        send_chunk(0, q, c)
        return nothing

    lax.fori_loop(0, chunks, first_chunk, 0)

    for copy in kap_sends:
        copy.wait_recv()

    def inside(axis, by):
        edge = 0 if by < 0 else size[axis] - 1
        return jnp.where(at[axis] == edge, 0.0, 1.0).astype(F32)

    def weights(x, nothing):
        own = [kp[x + 1, t * 8:(t + 1) * 8, :] for t in range(TILES)]
        x_low = jnp.where(x == 0, inside("gx", -1), 1.0)
        x_high = jnp.where(x == nx - 1, inside("gx", 1), 1.0)
        before = jnp.broadcast_to(kyr[0, pl.ds(x, 1), :] * inside("gy", -1), (8, 128))
        after = jnp.broadcast_to(kyr[1, pl.ds(x, 1), :] * inside("gy", 1), (8, 128))
        upper, lower = shifted_rows(own, before, after, row)
        turned = []
        for m in range(2):
            both = jnp.where(even, kzr[0, m] * inside("gz", -1), kzr[1, m] * inside("gz", 1))
            turned.append(pltpu.roll(both, lax.rem(128 - 2 * x, 128), 1))
        for t in range(TILES):
            pair = lane_roll(turned[t // 2], 127 - 64 * (t % 2))
            left, right = shifted_lanes(own[t], pair, lane)
            part = slice(t * 8, (t + 1) * 8)
            others = [
                kp[x + 2, part, :] * x_high, kp[x, part, :] * x_low,
                lower[t], upper[t], right, left,
            ]
            faces = [2.0 * own[t] * other * reciprocal(own[t] + other) for other in others]
            diagonal = faces[0]
            for face in faces[1:]:
                diagonal = diagonal + face
            scale = 2.5 * reciprocal(diagonal)
            for n in range(6):
                aa[x, n, part, :] = faces[n] * scale
        return nothing

    lax.fori_loop(0, nx, weights, 0, unroll=4)

    wide_lane = iota((16, 128), 1)
    second = jnp.where(iota((16, 128), 0) < 8, 0, TILES)
    groups = [((wide_lane >> 4) == second + t).astype(F32) for t in range(TILES)]

    for level in range(DEPTH):
        def chunk(q, nothing, level=level):
            c = order(q)
            for side in range(2):
                y_copy(level, side, c).wait_recv()
                z_copy(level, side, c).wait_recv()

            @pl.when(q == 1)
            def _():
                x_copy(level, 1).wait_recv()

            def outer_rows(i, nothing):
                x = c * CH + i
                for f in range(NF):
                    vv[level][x + 1, f, 7:8, :] = yr[level, 0, f, pl.ds(x, 1), :]
                    vv[level][x + 1, f, ny + 8:ny + 9, :] = yr[level, 1, f, pl.ds(x, 1), :]
                return nothing

            lax.fori_loop(0, CH, outer_rows, 0, unroll=4)
            columns = [[], []]
            for m in range(NF // 2):
                both = jnp.where(even, zr[level, 0, c, m], zr[level, 1, c, m])
                high = both.astype(BF16)
                low = (both - high.astype(F32)).astype(BF16)
                columns[0].append(jnp.concatenate([high, high], 0))
                columns[1].append(jnp.concatenate([low, low], 0))

            def unit(u, nothing):
                first = (CH // UNIT - 1 - u) * UNIT
                x0 = c * CH + first

                @pl.when((q == 0) & (u == CH // UNIT - 1))
                def _():
                    x_copy(level, 0).wait_recv()

                masks = []
                for i in range(UNIT):
                    mine = ((wide_lane >> 1) & (CH - 1)) == first + i
                    masks.append([jnp.where(mine, g, 0.0).astype(BF16) for g in groups])
                left_part = []
                for t in range(TILES):
                    outer = [
                        jnp.concatenate(
                            [columns[h][m] * masks[i][t] for i in range(UNIT) for m in range(NF // 2)], 0
                        )
                        for h in range(2)
                    ]
                    left_part.append(jnp.concatenate([halves(level, x0, UNIT, t)] + outer, 1))
                moved = jnp.dot(
                    jnp.concatenate(left_part, 0), shift[...], preferred_element_type=F32
                )
                for i in range(UNIT):
                    x = x0 + i
                    fields = []
                    for f in range(NF):
                        low = tiles_of(level, x, f)
                        high = tiles_of(level, x + 2, f)
                        upper = tiles_of(level, x + 1, f, -1)
                        lower = tiles_of(level, x + 1, f, 1)
                        tiles = []
                        for t in range(TILES):
                            at_row = ((t * UNIT + i) * NF + f) * 8
                            part = slice(t * 8, (t + 1) * 8)
                            total = aa[x, 0, part, :] * high[t]
                            total = total + aa[x, 1, part, :] * low[t]
                            total = total + aa[x, 2, part, :] * lower[t]
                            total = total + aa[x, 3, part, :] * upper[t]
                            total = total + aa[x, 4, part, :] * moved[at_row:at_row + 8, 128:]
                            total = total + aa[x, 5, part, :] * moved[at_row:at_row + 8, :128]
                            tiles.append(total)
                            if level + 1 < DEPTH:
                                vv[level + 1][x + 1, f, 8 + t * 8:16 + t * 8, :] = total
                        fields.append(tiles)
                    emit(level + 1, x, fields)
                if level + 1 < DEPTH:
                    @pl.when((q == 1) & (u == 0))
                    def _():
                        x_copy(level + 1, 0).start()

                return nothing

            lax.fori_loop(0, CH // UNIT, unit, 0)
            if level + 1 < DEPTH:
                send_chunk(level + 1, q, c)
            return nothing

        lax.fori_loop(0, chunks, chunk, 0)

    acc[...] = jnp.zeros_like(acc)

    def products(g, nothing):
        high, low = [
            jnp.concatenate(
                [
                    jnp.concatenate([ref[g * GROUP + i, h] for ref in hl], 0)
                    for i in range(GROUP)
                ],
                1,
            )
            for h in range(2)
        ]
        acc[...] += nt(jnp.concatenate([high, low], 0), high)
        return nothing

    lax.fori_loop(0, nx // GROUP, products, 0)

    same = (iota((ROWS, ROWS), 0) & 7) == (iota((ROWS, ROWS), 1) & 7)
    mixed = jnp.where(same, acc[0:ROWS] + 2.0 * acc[ROWS:], 0.0)
    pick_rows = ((iota((NC, ROWS), 1) >> 3) == iota((NC, ROWS), 0)).astype(F32)
    spread = ((iota((ROWS, 128), 0) >> 3) == iota((ROWS, 128), 1)).astype(F32)
    small = jnp.dot(pick_rows, mixed, precision=HIGH, preferred_element_type=F32)
    small = jnp.dot(small, spread, precision=HIGH, preferred_element_type=F32)
    message = small[0:8] + lane_roll(small[8:16], 32) + lane_roll(small[16:24], 64)

    sum_sends = []
    for number, count in enumerate((gx * gy, gz)):
        rank = ix * gy + iy if number == 0 else iz
        send, receive, slots = s_sem.at[number], r_sem.at[number], slot.at[number]

        def member(d):
            other = lax.rem(rank + d, count)
            if number:
                return other, {"gz": other}
            return other, {"gx": other // gy, "gy": lax.rem(other, gy)}

        msg[number] = message
        slots[rank] = message
        for d in range(1, count):
            copy = remote(
                msg.at[number], slots.at[rank], send.at[d], receive.at[rank], member(d)[1]
            )
            copy.start()
            sum_sends.append(copy)
        if number == 0:
            for copy in kap_sends:
                copy.wait_send()
            for level in range(DEPTH):
                for side in range(2):
                    x_copy(level, side).wait_send()

                    def drain(c, nothing, level=level, side=side):
                        y_copy(level, side, c).wait_send()
                        z_copy(level, side, c).wait_send()
                        return nothing

                    lax.fori_loop(0, chunks, drain, 0)
        for d in range(1, count):
            source, device = member(d)
            remote(msg.at[number], slots.at[source], send.at[d], receive.at[source], device).wait_recv()
        message = slots[0]
        for d in range(1, count):
            message = message + slots[d]

    message = message * (0.5 / cells)
    lanes = iota((NC, 128), 1)
    rows = iota((NC, 128), 0)
    parts = [message, lane_roll(message, 96), lane_roll(message, 64)]
    half = jnp.where(lanes < NC, jnp.concatenate(parts, 0), 0.0)
    identity = (lanes == rows).astype(F32)
    padded = jnp.concatenate([half, jnp.zeros((128 - NC, 128), F32)], 0)
    matrix = half + nt(identity, padded, HIGH) + (lanes == rows + 32).astype(F32)
    pivots = jnp.ones((NC, 128), F32)

    def across(value, k):
        return jnp.broadcast_to(value[k:k + 1, :], (NC, 128))

    for first in range(0, NC, NF):
        columns = [
            jnp.broadcast_to(matrix[:, k:k + 1], (NC, 128)) for k in range(first, first + NF)
        ]
        for j in range(NF):
            k = first + j
            pivot = across(columns[j], k)
            pivots = jnp.where(rows == k, pivot, pivots)
            factors = jnp.where(rows > k, columns[j] * reciprocal(pivot), 0.0)
            for later in range(j + 1, NF):
                columns[later] = columns[later] - factors * across(columns[j], first + later)
            matrix = matrix - factors * across(matrix, k)
    matrix = matrix * (1.0 / jnp.sqrt(pivots))
    factor[...] = jnp.where((lanes >= rows) & (lanes < NC), matrix, 0.0)
    inverse = jnp.where(lanes <= rows, lane_roll(matrix, 96), 0.0)

    padded = jnp.concatenate([inverse, jnp.zeros((128 - NC, 128), F32)], 0)
    high = padded.astype(BF16).astype(F32)
    both = (high + lane_roll((padded - high).astype(BF16).astype(F32), NC)).astype(BF16)
    tall = jnp.dot(spread.astype(BF16), both, preferred_element_type=F32).astype(BF16)
    place, chosen = iota((3 * ROWS, 128), 0), iota((3 * ROWS, 128), 1)
    kind = (place >= 3 * BAND).astype(jnp.int32)
    for level in range(2, LEVELS):
        kind = kind + (place >= 3 * BAND * level).astype(jnp.int32)
    inner = place - 3 * BAND * kind
    place = kind * BAND + jnp.where(
        inner < BAND, inner, jnp.where(inner < 2 * BAND, inner - BAND, inner - 2 * BAND + ROWS)
    )
    wide = nt(tall, ((place >> 3) == chosen).astype(F32).astype(BF16))
    same = (iota((ROWS, 3 * ROWS), 0) & 7) == (iota((ROWS, 3 * ROWS), 1) & 7)
    wmat[...] = jnp.where(same, wide, 0.0).astype(BF16)

    for copy in sum_sends:
        copy.wait_send()


def solve_kernel(wmat, factor, hl0, hl1, hl2, hl3, q, r, held, sems):
    nx = hl0.shape[0]
    r[...] = factor[:, 0:NC]

    steps = nx // SPAN

    def out_copy(g):
        slot = lax.rem(g, SLOTS)
        return pltpu.make_async_copy(held.at[slot], q.at[:, pl.ds(g * SPAN, SPAN)], sems.at[slot])

    def planes(g, nothing):
        @pl.when(g >= SLOTS)
        def _():
            out_copy(g - SLOTS).wait()

        slot = lax.rem(g, SLOTS)
        data = []
        for ref in (hl0, hl1, hl2, hl3):
            high, low = [
                jnp.concatenate([ref[g * SPAN + i, h] for i in range(SPAN)], 1) for h in range(2)
            ]
            data += [high, low, high]
        data = jnp.concatenate(data, 0)
        result = None
        for start in range(0, 3 * ROWS, 256):
            stop = min(start + 256, 3 * ROWS)
            above = start // (3 * BAND) * BAND
            part = jnp.dot(
                wmat[above:, start:stop], data[start:stop], preferred_element_type=F32
            )
            if result is not None:
                part = jnp.concatenate([result[:above], result[above:] + part], 0)
            result = part
        for f in range(NC):
            for i in range(SPAN):
                for t in range(TILES):
                    col = (i * TILES + t) * 128
                    held[slot, f, i, t * 8:(t + 1) * 8, :] = result[f * 8:(f + 1) * 8, col:col + 128]
        out_copy(g).start()
        return nothing

    lax.fori_loop(0, steps, planes, 0)

    def drain(g, nothing):
        out_copy(g).wait()
        return nothing

    lax.fori_loop(max(steps - SLOTS, 0), steps, drain, 0)


def on_device(sizes, right_sides, permeability):
    nx, ny, nz = permeability.shape
    chunks = nx // CH
    cells = float(nx * ny * nz * sizes[0] * sizes[1] * sizes[2])
    most = max(sizes[0] * sizes[1], sizes[2])
    dma = pltpu.SemaphoreType.DMA
    vmem = pl.BlockSpec(memory_space=pltpu.VMEM)
    *hl, wmat, factor = pl.pallas_call(
        functools.partial(basis_kernel, sizes, cells),
        out_shape=(
            *[pltpu.VMEM((nx, 2, BAND, TILES * 128), BF16)] * LEVELS,
            pltpu.VMEM((ROWS, 3 * ROWS), BF16),
            pltpu.VMEM((NC, 128), F32),
        ),
        in_specs=[pl.BlockSpec(memory_space=pl.ANY)] * 2,
        out_specs=(vmem,) * (LEVELS + 2),
        scratch_shapes=[
            pltpu.VMEM((nx + 2, ny, 128), F32),
            pltpu.VMEM((2, nx, 128), F32),
            pltpu.VMEM((2, nx, 128), F32),
            pltpu.VMEM((2, 8, 128), F32),
            pltpu.VMEM((2, 2, 8, 128), F32),
            *[pltpu.VMEM((nx + 2, NF, ny + 16, 128), F32)] * DEPTH,
            pltpu.VMEM((nx, 6, ny, 128), F32),
            pltpu.VMEM((DEPTH, 2, NF, nx, 128), F32),
            pltpu.VMEM((DEPTH, 2, NF, nx, 128), F32),
            pltpu.VMEM((DEPTH, chunks, NF // 2, 8, 128), F32),
            pltpu.VMEM((DEPTH, 2, chunks, NF // 2, 8, 128), F32),
            pltpu.VMEM((512, 256), BF16),
            pltpu.VMEM((256, 128), BF16),
            pltpu.VMEM((2 * ROWS, ROWS), F32),
            pltpu.VMEM((2, 8, 128), F32),
            pltpu.VMEM((2, most, 8, 128), F32),
            dma((NF + 1,)),
            dma((6,)), dma((6,)),
            dma((DEPTH, 2)), dma((DEPTH, 2)),
            dma((DEPTH, 2, chunks)), dma((DEPTH, 2, chunks)),
            dma((DEPTH, 2, chunks)), dma((DEPTH, 2, chunks)),
            dma((2, most)), dma((2, most)),
        ],
        compiler_params=pltpu.CompilerParams(
            collective_id=0, has_side_effects=True, vmem_limit_bytes=44 * 1024 * 1024
        ),
        name="basis",
    )(right_sides, permeability)
    return pl.pallas_call(
        solve_kernel,
        out_shape=(
            jax.ShapeDtypeStruct((NC, nx, ny, 128), F32),
            jax.ShapeDtypeStruct((NC, NC), F32),
        ),
        in_specs=[vmem] * (LEVELS + 2),
        out_specs=(pl.BlockSpec(memory_space=pl.ANY), vmem),
        scratch_shapes=[
            pltpu.VMEM((SLOTS, NC, SPAN, ny, 128), F32),
            dma((SLOTS,)),
        ],
        compiler_params=pltpu.CompilerParams(vmem_limit_bytes=12 * 1024 * 1024),
        name="solve",
    )(wmat, factor, *hl)


def solution(mesh):
    sizes = tuple(mesh.shape[axis] for axis in ("gx", "gy", "gz"))
    return jax.shard_map(
        functools.partial(on_device, sizes),
        mesh=mesh,
        in_specs=(P(None, "gx", "gy", "gz"), P("gx", "gy", "gz")),
        out_specs=(P(None, "gx", "gy", "gz"), P()),
        check_vma=False,
    )
```

```python
import functools

import jax
import jax.numpy as jnp
from jax import lax
from jax.experimental import pallas as pl
from jax.experimental.pallas import tpu as pltpu
from jax.sharding import PartitionSpec as P

NF = 6
DEPTH = 3
LEVELS = DEPTH + 1
NC = NF * LEVELS
CH = 8
TILES = 4
ROWS = NC * 8
BAND = NF * 8
UNIT = 4
GROUP = 8
SPAN = 4
SLOTS = 4
MESH = pl.DeviceIdType.MESH
F32 = jnp.float32
BF16 = jnp.bfloat16
HIGH = lax.Precision.HIGHEST


def iota(shape, dim):
    return lax.broadcasted_iota(jnp.int32, shape, dim)


def nt(left, right, precision=None):
    return lax.dot_general(
        left, right, (((1,), (1,)), ((), ())), precision=precision, preferred_element_type=F32
    )


def reciprocal(value):
    guess = pl.reciprocal(value, approx=True)
    return guess * (2.0 - value * guess)


def lane_roll(value, amount):
    return pltpu.roll(value, amount % 128, 1)


def shifted_rows(tiles, before, after, row):
    rolled = [pltpu.roll(v, 1, 0) for v in tiles]
    upper = [jnp.where(row == 0, p, r) for p, r in zip([before] + rolled[:-1], rolled)]
    rolled = [pltpu.roll(v, 7, 0) for v in tiles]
    lower = [jnp.where(row == 7, n, r) for n, r in zip(rolled[1:] + [after], rolled)]
    return upper, lower


def shifted_lanes(value, pair, lane):
    left = lane_roll(jnp.where(lane == 127, pair, value), 1)
    right = lane_roll(jnp.where(lane == 0, pair, value), 127)
    return left, right


def basis_kernel(
    sizes, cells, rs, kap, hl0, hl1, hl2, hl3, wmat, factor,
    kp, kys, kyr, kzs, kzr, v0, v1, v2, aa, ys, yr, zs, zr, shift, gather, acc, msg, slot,
    load_sem, ks_sem, kr_sem, xs_sem, xr_sem, ys_sem, yr_sem, zs_sem, zr_sem,
    s_sem, r_sem,
):
    hl = (hl0, hl1, hl2, hl3)
    vv = (v0, v1, v2)
    gx, gy, gz = sizes
    nx, ny = kp.shape[0] - 2, kp.shape[1]
    chunks = nx // CH
    ix, iy, iz = lax.axis_index("gx"), lax.axis_index("gy"), lax.axis_index("gz")
    at = {"gx": ix, "gy": iy, "gz": iz}
    size = {"gx": gx, "gy": gy, "gz": gz}

    def toward(axis, by):
        return {axis: lax.rem(at[axis] + (by + size[axis]), size[axis])}

    kap_copy = pltpu.make_async_copy(kap, kp.at[pl.ds(1, nx)], load_sem.at[NF])
    kap_copy.start()
    field_copies = []
    for f in range(NF):
        copy = pltpu.make_async_copy(rs.at[f], v0.at[pl.ds(1, nx), f, pl.ds(8, ny)], load_sem.at[f])
        copy.start()
        field_copies.append(copy)

    n1 = gx * gy
    rank1 = ix * gy + iy
    barrier = pltpu.get_barrier_semaphore()
    greeted = []
    for d in range(1, n1):
        other = lax.rem(rank1 + d, n1)
        greeted.append({"gx": other // gy, "gy": lax.rem(other, gy)})
    greeted += [{"gz": lax.rem(iz + d, gz)} for d in range(1, gz)]
    for device in greeted:
        pl.semaphore_signal(barrier, inc=1, device_id=device, device_id_type=MESH)

    lane = iota((8, 128), 1)
    row = iota((8, 128), 0)
    even = (lane & 1) == 0
    zero = jnp.zeros((8, 128), F32)

    def remote(src, dst, send, recv, device):
        return pltpu.make_async_remote_copy(
            src_ref=src, dst_ref=dst, send_sem=send, recv_sem=recv,
            device_id=device, device_id_type=MESH,
        )

    source, target = iota((256, 256), 0) & 127, iota((256, 256), 1)
    wanted = jnp.where(target < 128, target - 1, target - 127)
    shift[0:256] = (source == wanted).astype(F32).astype(BF16)
    wanted = jnp.where((source & 1) == 0, 0, 255)
    shift[256:512] = (target == wanted).astype(F32).astype(BF16)
    source, target = iota((256, 128), 0) & 127, iota((256, 128), 1)
    wanted = jnp.where((target & 1) == 0, 127, 0)
    gather[...] = (source == wanted).astype(F32).astype(BF16)

    kap_copy.wait()

    def pack_kap(x, carry):
        tiles = [kp[x + 1, t * 8:(t + 1) * 8, :] for t in range(TILES)]
        kys[0, pl.ds(x, 1), :] = tiles[0][0:1]
        kys[1, pl.ds(x, 1), :] = tiles[3][7:8]
        result = []
        for m in range(2):
            both = jnp.where(lane < 64, lane_roll(tiles[2 * m], 1), lane_roll(tiles[2 * m + 1], 65))
            both = pltpu.roll(both, 2 * x, 1)
            result.append(jnp.where(((lane >> 1) & 31) == x, both, carry[m]))
        return tuple(result)

    packed = lax.fori_loop(0, nx, pack_kap, (zero, zero), unroll=8)
    for m in range(2):
        kzs[m] = packed[m]
    pl.semaphore_wait(barrier, n1 + gz - 2)

    kap_sends = [
        remote(kp.at[nx], kp.at[0], ks_sem.at[0], kr_sem.at[0], toward("gx", 1)),
        remote(kp.at[1], kp.at[nx + 1], ks_sem.at[1], kr_sem.at[1], toward("gx", -1)),
        remote(kys.at[1], kyr.at[0], ks_sem.at[2], kr_sem.at[2], toward("gy", 1)),
        remote(kys.at[0], kyr.at[1], ks_sem.at[3], kr_sem.at[3], toward("gy", -1)),
        remote(kzs, kzr.at[0], ks_sem.at[4], kr_sem.at[4], toward("gz", 1)),
        remote(kzs, kzr.at[1], ks_sem.at[5], kr_sem.at[5], toward("gz", -1)),
    ]
    for copy in kap_sends:
        copy.start()

    def x_copy(level, side):
        src, dst = (nx, 0) if side == 0 else (1, nx + 1)
        return remote(
            vv[level].at[src, :, pl.ds(8, ny)], vv[level].at[dst, :, pl.ds(8, ny)], xs_sem.at[level, side], xr_sem.at[level, side],
            toward("gx", 1 - 2 * side),
        )

    def y_copy(level, side, c):
        part = pl.ds(pl.multiple_of(c * CH, CH), CH)
        return remote(
            ys.at[level, 1 - side, :, part, :], yr.at[level, side, :, part, :],
            ys_sem.at[level, side, c], yr_sem.at[level, side, c], toward("gy", 1 - 2 * side),
        )

    def z_copy(level, side, c):
        return remote(
            zs.at[level, c], zr.at[level, side, c],
            zs_sem.at[level, side, c], zr_sem.at[level, side, c], toward("gz", 1 - 2 * side),
        )

    def emit(level, x, fields):
        for f in range(0, NF, 2):
            for t in range(TILES):
                full = jnp.concatenate([fields[f][t], fields[f + 1][t]], 0)
                high = full.astype(BF16)
                low = (full - high.astype(F32)).astype(BF16)
                hl[level][x, 0, f * 8:f * 8 + 16, t * 128:(t + 1) * 128] = high
                hl[level][x, 1, f * 8:f * 8 + 16, t * 128:(t + 1) * 128] = low
        if level < DEPTH:
            for f in range(NF):
                ys[level, 0, f, pl.ds(x, 1), :] = fields[f][0][0:1]
                ys[level, 1, f, pl.ds(x, 1), :] = fields[f][TILES - 1][7:8]

    def halves(level, x, count, t):
        part = slice(t * 128, (t + 1) * 128)
        return jnp.concatenate(
            [hl[level][pl.ds(x, count), h, :, part].reshape(count * BAND, 128) for h in range(2)], 1
        )

    def pack_chunk(level, c):
        result = [zero] * (NF // 2)
        for t in range(TILES):
            outer = jnp.dot(
                halves(level, c * CH, CH, t), gather[...], preferred_element_type=F32
            )
            for i in range(CH):
                for f in range(NF):
                    at_row = (i * NF + f) * 8
                    mask = (lane >> 1) == ((f % 2) * TILES + t) * CH + i
                    result[f // 2] = jnp.where(mask, outer[at_row:at_row + 8], result[f // 2])
        for m in range(NF // 2):
            zs[level, c, m] = result[m]

    def send_chunk(level, q, c):
        for side in range(2):
            y_copy(level, side, c).start()
        if level > 0:
            @pl.when(q == 0)
            def _():
                x_copy(level, 1).start()

        pack_chunk(level, c)
        for side in range(2):
            z_copy(level, side, c).start()

    def tiles_of(level, plane, f, by=0):
        return [vv[level][plane, f, pl.ds(8 + by + t * 8, 8), :] for t in range(TILES)]

    def order(q):
        return lax.rem(q * (chunks - 1), chunks)

    for copy in field_copies:
        copy.wait()
    for side in range(2):
        x_copy(0, side).start()

    def first_chunk(q, nothing):
        c = order(q)

        def plane(i, nothing):
            x = c * CH + i
            emit(0, x, [tiles_of(0, x + 1, f) for f in range(NF)])
            return nothing

        lax.fori_loop(0, CH, plane, 0, unroll=4)
        send_chunk(0, q, c)
        return nothing

    lax.fori_loop(0, chunks, first_chunk, 0)

    for copy in kap_sends:
        copy.wait_recv()

    def inside(axis, by):
        edge = 0 if by < 0 else size[axis] - 1
        return jnp.where(at[axis] == edge, 0.0, 1.0).astype(F32)

    def weights(x, nothing):
        own = [kp[x + 1, t * 8:(t + 1) * 8, :] for t in range(TILES)]
        x_low = jnp.where(x == 0, inside("gx", -1), 1.0)
        x_high = jnp.where(x == nx - 1, inside("gx", 1), 1.0)
        before = jnp.broadcast_to(kyr[0, pl.ds(x, 1), :] * inside("gy", -1), (8, 128))
        after = jnp.broadcast_to(kyr[1, pl.ds(x, 1), :] * inside("gy", 1), (8, 128))
        upper, lower = shifted_rows(own, before, after, row)
        turned = []
        for m in range(2):
            both = jnp.where(even, kzr[0, m] * inside("gz", -1), kzr[1, m] * inside("gz", 1))
            turned.append(pltpu.roll(both, lax.rem(128 - 2 * x, 128), 1))
        for t in range(TILES):
            pair = lane_roll(turned[t // 2], 127 - 64 * (t % 2))
            left, right = shifted_lanes(own[t], pair, lane)
            part = slice(t * 8, (t + 1) * 8)
            others = [
                kp[x + 2, part, :] * x_high, kp[x, part, :] * x_low,
                lower[t], upper[t], right, left,
            ]
            faces = [2.0 * own[t] * other * reciprocal(own[t] + other) for other in others]
            diagonal = faces[0]
            for face in faces[1:]:
                diagonal = diagonal + face
            scale = 2.5 * reciprocal(diagonal)
            for n in range(6):
                aa[x, n, part, :] = faces[n] * scale
        return nothing

    lax.fori_loop(0, nx, weights, 0, unroll=8)

    wide_lane = iota((16, 128), 1)
    second = jnp.where(iota((16, 128), 0) < 8, 0, TILES)
    groups = [((wide_lane >> 4) == second + t).astype(F32) for t in range(TILES)]

    for level in range(DEPTH):
        def chunk(q, nothing, level=level):
            c = order(q)
            for side in range(2):
                y_copy(level, side, c).wait_recv()
                z_copy(level, side, c).wait_recv()

            @pl.when(q == 1)
            def _():
                x_copy(level, 1).wait_recv()

            def outer_rows(i, nothing):
                x = c * CH + i
                for f in range(NF):
                    vv[level][x + 1, f, 7:8, :] = yr[level, 0, f, pl.ds(x, 1), :]
                    vv[level][x + 1, f, ny + 8:ny + 9, :] = yr[level, 1, f, pl.ds(x, 1), :]
                return nothing

            lax.fori_loop(0, CH, outer_rows, 0, unroll=4)
            columns = [[], []]
            for m in range(NF // 2):
                both = jnp.where(even, zr[level, 0, c, m], zr[level, 1, c, m])
                high = both.astype(BF16)
                low = (both - high.astype(F32)).astype(BF16)
                columns[0].append(jnp.concatenate([high, high], 0))
                columns[1].append(jnp.concatenate([low, low], 0))

            def unit(u, nothing):
                first = (CH // UNIT - 1 - u) * UNIT
                x0 = c * CH + first

                @pl.when((q == 0) & (u == CH // UNIT - 1))
                def _():
                    x_copy(level, 0).wait_recv()

                masks = []
                for i in range(UNIT):
                    mine = ((wide_lane >> 1) & (CH - 1)) == first + i
                    masks.append([jnp.where(mine, g, 0.0).astype(BF16) for g in groups])
                left_part = []
                for t in range(TILES):
                    outer = [
                        jnp.concatenate(
                            [columns[h][m] * masks[i][t] for i in range(UNIT) for m in range(NF // 2)], 0
                        )
                        for h in range(2)
                    ]
                    left_part.append(jnp.concatenate([halves(level, x0, UNIT, t)] + outer, 1))
                moved = jnp.dot(
                    jnp.concatenate(left_part, 0), shift[...], preferred_element_type=F32
                )
                for i in range(UNIT):
                    x = x0 + i
                    fields = []
                    for f in range(NF):
                        low = tiles_of(level, x, f)
                        high = tiles_of(level, x + 2, f)
                        upper = tiles_of(level, x + 1, f, -1)
                        lower = tiles_of(level, x + 1, f, 1)
                        tiles = []
                        for t in range(TILES):
                            at_row = ((t * UNIT + i) * NF + f) * 8
                            part = slice(t * 8, (t + 1) * 8)
                            total = aa[x, 0, part, :] * high[t]
                            total = total + aa[x, 1, part, :] * low[t]
                            total = total + aa[x, 2, part, :] * lower[t]
                            total = total + aa[x, 3, part, :] * upper[t]
                            total = total + aa[x, 4, part, :] * moved[at_row:at_row + 8, 128:]
                            total = total + aa[x, 5, part, :] * moved[at_row:at_row + 8, :128]
                            tiles.append(total)
                            if level + 1 < DEPTH:
                                vv[level + 1][x + 1, f, 8 + t * 8:16 + t * 8, :] = total
                        fields.append(tiles)
                    emit(level + 1, x, fields)
                if level + 1 < DEPTH:
                    @pl.when((q == 1) & (u == 0))
                    def _():
                        x_copy(level + 1, 0).start()

                return nothing

            lax.fori_loop(0, CH // UNIT, unit, 0)
            if level + 1 < DEPTH:
                send_chunk(level + 1, q, c)
            return nothing

        lax.fori_loop(0, chunks, chunk, 0)

    acc[...] = jnp.zeros_like(acc)

    def products(g, nothing):
        high, low = [
            jnp.concatenate(
                [
                    jnp.concatenate([ref[g * GROUP + i, h] for ref in hl], 0)
                    for i in range(GROUP)
                ],
                1,
            )
            for h in range(2)
        ]
        acc[...] += nt(jnp.concatenate([high, low], 0), high)
        return nothing

    lax.fori_loop(0, nx // GROUP, products, 0)

    same = (iota((ROWS, ROWS), 0) & 7) == (iota((ROWS, ROWS), 1) & 7)
    mixed = jnp.where(same, acc[0:ROWS] + 2.0 * acc[ROWS:], 0.0)
    pick_rows = ((iota((NC, ROWS), 1) >> 3) == iota((NC, ROWS), 0)).astype(F32)
    spread = ((iota((ROWS, 128), 0) >> 3) == iota((ROWS, 128), 1)).astype(F32)
    small = jnp.dot(pick_rows, mixed, precision=HIGH, preferred_element_type=F32)
    small = jnp.dot(small, spread, precision=HIGH, preferred_element_type=F32)
    message = small[0:8] + lane_roll(small[8:16], 32) + lane_roll(small[16:24], 64)

    sum_sends = []
    for number, count in enumerate((gx * gy, gz)):
        rank = ix * gy + iy if number == 0 else iz
        send, receive, slots = s_sem.at[number], r_sem.at[number], slot.at[number]

        def member(d):
            other = lax.rem(rank + d, count)
            if number:
                return other, {"gz": other}
            return other, {"gx": other // gy, "gy": lax.rem(other, gy)}

        msg[number] = message
        slots[rank] = message
        for d in range(1, count):
            copy = remote(
                msg.at[number], slots.at[rank], send.at[d], receive.at[rank], member(d)[1]
            )
            copy.start()
            sum_sends.append(copy)
        if number == 0:
            for copy in kap_sends:
                copy.wait_send()
            for level in range(DEPTH):
                for side in range(2):
                    x_copy(level, side).wait_send()

                    def drain(c, nothing, level=level, side=side):
                        y_copy(level, side, c).wait_send()
                        z_copy(level, side, c).wait_send()
                        return nothing

                    lax.fori_loop(0, chunks, drain, 0)
        for d in range(1, count):
            source, device = member(d)
            remote(msg.at[number], slots.at[source], send.at[d], receive.at[source], device).wait_recv()
        message = slots[0]
        for d in range(1, count):
            message = message + slots[d]

    message = message * (0.5 / cells)
    lanes = iota((NC, 128), 1)
    rows = iota((NC, 128), 0)
    parts = [message, lane_roll(message, 96), lane_roll(message, 64)]
    half = jnp.where(lanes < NC, jnp.concatenate(parts, 0), 0.0)
    identity = (lanes == rows).astype(F32)
    padded = jnp.concatenate([half, jnp.zeros((128 - NC, 128), F32)], 0)
    matrix = half + nt(identity, padded, HIGH) + (lanes == rows + 32).astype(F32)
    pivots = jnp.ones((NC, 128), F32)

    def across(value, k):
        return jnp.broadcast_to(value[k:k + 1, :], (NC, 128))

    for first in range(0, NC, NF):
        columns = [
            jnp.broadcast_to(matrix[:, k:k + 1], (NC, 128)) for k in range(first, first + NF)
        ]
        for j in range(NF):
            k = first + j
            pivot = across(columns[j], k)
            pivots = jnp.where(rows == k, pivot, pivots)
            factors = jnp.where(rows > k, columns[j] * reciprocal(pivot), 0.0)
            for later in range(j + 1, NF):
                columns[later] = columns[later] - factors * across(columns[j], first + later)
            matrix = matrix - factors * across(matrix, k)
    matrix = matrix * (1.0 / jnp.sqrt(pivots))
    factor[...] = jnp.where((lanes >= rows) & (lanes < NC), matrix, 0.0)
    inverse = jnp.where(lanes <= rows, lane_roll(matrix, 96), 0.0)

    padded = jnp.concatenate([inverse, jnp.zeros((128 - NC, 128), F32)], 0)
    high = padded.astype(BF16).astype(F32)
    both = (high + lane_roll((padded - high).astype(BF16).astype(F32), NC)).astype(BF16)
    tall = jnp.dot(spread.astype(BF16), both, preferred_element_type=F32).astype(BF16)
    place, chosen = iota((3 * ROWS, 128), 0), iota((3 * ROWS, 128), 1)
    kind = (place >= 3 * BAND).astype(jnp.int32)
    for level in range(2, LEVELS):
        kind = kind + (place >= 3 * BAND * level).astype(jnp.int32)
    inner = place - 3 * BAND * kind
    place = kind * BAND + jnp.where(
        inner < BAND, inner, jnp.where(inner < 2 * BAND, inner - BAND, inner - 2 * BAND + ROWS)
    )
    wide = nt(tall, ((place >> 3) == chosen).astype(F32).astype(BF16))
    same = (iota((ROWS, 3 * ROWS), 0) & 7) == (iota((ROWS, 3 * ROWS), 1) & 7)
    wmat[...] = jnp.where(same, wide, 0.0).astype(BF16)

    for copy in sum_sends:
        copy.wait_send()


def solve_kernel(wmat, factor, hl0, hl1, hl2, hl3, q, r, held, sems):
    nx = hl0.shape[0]
    r[...] = factor[:, 0:NC]

    steps = nx // SPAN

    def out_copy(g):
        slot = lax.rem(g, SLOTS)
        return pltpu.make_async_copy(held.at[slot], q.at[:, pl.ds(g * SPAN, SPAN)], sems.at[slot])

    def planes(g, nothing):
        @pl.when(g >= SLOTS)
        def _():
            out_copy(g - SLOTS).wait()

        slot = lax.rem(g, SLOTS)
        data = []
        for ref in (hl0, hl1, hl2, hl3):
            high, low = [
                jnp.concatenate([ref[g * SPAN + i, h] for i in range(SPAN)], 1) for h in range(2)
            ]
            data += [high, low, high]
        data = jnp.concatenate(data, 0)
        result = None
        for start in range(0, 3 * ROWS, 256):
            stop = min(start + 256, 3 * ROWS)
            above = start // (3 * BAND) * BAND
            part = jnp.dot(
                wmat[above:, start:stop], data[start:stop], preferred_element_type=F32
            )
            if result is not None:
                part = jnp.concatenate([result[:above], result[above:] + part], 0)
            result = part
        for f in range(NC):
            for i in range(SPAN):
                for t in range(TILES):
                    col = (i * TILES + t) * 128
                    held[slot, f, i, t * 8:(t + 1) * 8, :] = result[f * 8:(f + 1) * 8, col:col + 128]
        out_copy(g).start()
        return nothing

    lax.fori_loop(0, steps, planes, 0)

    def drain(g, nothing):
        out_copy(g).wait()
        return nothing

    lax.fori_loop(max(steps - SLOTS, 0), steps, drain, 0)


def on_device(sizes, right_sides, permeability):
    nx, ny, nz = permeability.shape
    chunks = nx // CH
    cells = float(nx * ny * nz * sizes[0] * sizes[1] * sizes[2])
    most = max(sizes[0] * sizes[1], sizes[2])
    dma = pltpu.SemaphoreType.DMA
    vmem = pl.BlockSpec(memory_space=pltpu.VMEM)
    *hl, wmat, factor = pl.pallas_call(
        functools.partial(basis_kernel, sizes, cells),
        out_shape=(
            *[pltpu.VMEM((nx, 2, BAND, TILES * 128), BF16)] * LEVELS,
            pltpu.VMEM((ROWS, 3 * ROWS), BF16),
            pltpu.VMEM((NC, 128), F32),
        ),
        in_specs=[pl.BlockSpec(memory_space=pl.ANY)] * 2,
        out_specs=(vmem,) * (LEVELS + 2),
        scratch_shapes=[
            pltpu.VMEM((nx + 2, ny, 128), F32),
            pltpu.VMEM((2, nx, 128), F32),
            pltpu.VMEM((2, nx, 128), F32),
            pltpu.VMEM((2, 8, 128), F32),
            pltpu.VMEM((2, 2, 8, 128), F32),
            *[pltpu.VMEM((nx + 2, NF, ny + 16, 128), F32)] * DEPTH,
            pltpu.VMEM((nx, 6, ny, 128), F32),
            pltpu.VMEM((DEPTH, 2, NF, nx, 128), F32),
            pltpu.VMEM((DEPTH, 2, NF, nx, 128), F32),
            pltpu.VMEM((DEPTH, chunks, NF // 2, 8, 128), F32),
            pltpu.VMEM((DEPTH, 2, chunks, NF // 2, 8, 128), F32),
            pltpu.VMEM((512, 256), BF16),
            pltpu.VMEM((256, 128), BF16),
            pltpu.VMEM((2 * ROWS, ROWS), F32),
            pltpu.VMEM((2, 8, 128), F32),
            pltpu.VMEM((2, most, 8, 128), F32),
            dma((NF + 1,)),
            dma((6,)), dma((6,)),
            dma((DEPTH, 2)), dma((DEPTH, 2)),
            dma((DEPTH, 2, chunks)), dma((DEPTH, 2, chunks)),
            dma((DEPTH, 2, chunks)), dma((DEPTH, 2, chunks)),
            dma((2, most)), dma((2, most)),
        ],
        compiler_params=pltpu.CompilerParams(
            collective_id=0, has_side_effects=True, vmem_limit_bytes=44 * 1024 * 1024
        ),
        name="basis",
    )(right_sides, permeability)
    return pl.pallas_call(
        solve_kernel,
        out_shape=(
            jax.ShapeDtypeStruct((NC, nx, ny, 128), F32),
            jax.ShapeDtypeStruct((NC, NC), F32),
        ),
        in_specs=[vmem] * (LEVELS + 2),
        out_specs=(pl.BlockSpec(memory_space=pl.ANY), vmem),
        scratch_shapes=[
            pltpu.VMEM((SLOTS, NC, SPAN, ny, 128), F32),
            dma((SLOTS,)),
        ],
        compiler_params=pltpu.CompilerParams(vmem_limit_bytes=12 * 1024 * 1024),
        name="solve",
    )(wmat, factor, *hl)


def solution(mesh):
    sizes = tuple(mesh.shape[axis] for axis in ("gx", "gy", "gz"))
    return jax.shard_map(
        functools.partial(on_device, sizes),
        mesh=mesh,
        in_specs=(P(None, "gx", "gy", "gz"), P("gx", "gy", "gz")),
        out_specs=(P(None, "gx", "gy", "gz"), P()),
        check_vma=False,
    )
```
